128 devices in a mesh: dp: 32 (over z_lo, x, y), mp: 4 (over z_hi, core).
Axes of the slice: x: 4, y: 4, z: 4 (z_hi: 2, z_lo: 2; z = z_hi * 2 + z_lo), core: 2. Of those that a mesh axis runs over, the one named last changes fastest.
Arguments:
- image_feats: bfloat16 [16384, 1152], P(('dp', 'mp')), may hold values from -6 to 6
- text_feats: bfloat16 [16384, 1152], P(('dp', 'mp')), may hold values from -6 to 6
- image_proj: bfloat16 [1152, 1152], replicated, may hold values from -0.1875 to 0.1875
- text_proj: bfloat16 [1152, 1152], replicated, may hold values from -0.1875 to 0.1875
- log_scale: float32 [1], replicated, may hold values from 3.6 to 4.3
- logit_bias: float32 [1], replicated, may hold values from -12 to -9
Outputs:
- loss: float32 [1], replicated
- image_proj_grad: float32 [1152, 1152], P(('dp', 'mp'))
- text_proj_grad: float32 [1152, 1152], P(('dp', 'mp'))
- log_scale_grad: float32 [1], replicated
- bias_grad: float32 [1], replicated
The draws below stay inside these ranges and needn't reach their ends.
All inputs are finite; a program needn't handle non-finite values.
Results may differ from the reference program's by a relative error of at most 0.0035.
Values may be sent and summed in bfloat16 or wider, within the bound.
A program may use at most 128 MiB of HBM per device.

```python
import math
import jax
import jax.numpy as jnp
from jax import lax

WIDTH = 1152
BATCH = 16384


def steps_of(stream_key, dims, cuts, low, top_value):
    level = 1.0
    for dim, blocks in cuts:
        heights = jax.random.uniform(jax.random.fold_in(jax.random.fold_in(stream_key, 6), dim), (blocks,), jnp.float32, low / len(cuts), top_value / len(cuts))
        level = level * jnp.repeat(jnp.exp(heights), dims[dim] // blocks).reshape((-1,) + (1,) * (len(dims) - 1 - dim))
    return level


def normal_values(stream_key, shape, deviation, limit, shards=(), kind=jnp.bfloat16):
    loudness = steps_of(stream_key, shape, shards, -0.22, 0.18) if shards else 1.0
    drawn = jax.random.normal(stream_key, shape, jnp.float32) * deviation * loudness
    return jnp.minimum(jnp.maximum(drawn, -limit), limit).astype(kind)


def setup_inputs(seed: int = 0) -> dict:
    streams_of = jax.random.split(jax.random.key(seed), 7)
    return {
        "image_feats": normal_values(streams_of[0], (BATCH, WIDTH), 1.0, 6.0, ((0, 128),)),
        "text_feats": normal_values(streams_of[1], (BATCH, WIDTH), 1.0, 6.0, ((0, 128),)),
        "image_proj": normal_values(streams_of[2], (WIDTH, WIDTH), WIDTH ** -0.5, 0.1875),
        "text_proj": normal_values(streams_of[3], (WIDTH, WIDTH), WIDTH ** -0.5, 0.1875),
        "log_scale": jnp.clip(jax.random.uniform(streams_of[4], (1,), jnp.float32, 3.6, 4.3), 3.6, 4.3),
        "logit_bias": jnp.clip(jax.random.uniform(streams_of[5], (1,), jnp.float32, -12.0, -9.0), -12.0, -9.0),
    }


def normalize(features, projection):
    projected = jnp.dot(features, projection, preferred_element_type=jnp.float32)
    row_norm = jnp.sqrt(lax.optimization_barrier(jnp.sum(projected * projected, axis=-1, keepdims=True)) + 1e-06)
    return (projected / row_norm, row_norm)

def unnormalize(unit_rows, row_norm, unit_grad):
    inner_product = lax.optimization_barrier(jnp.sum(unit_rows * unit_grad, axis=-1, keepdims=True))
    return ((unit_grad - unit_rows * inner_product) / row_norm).astype(jnp.bfloat16)

def pair_terms(cosine, label_signs, logit_scale, bias_value):
    logits = logit_scale * cosine + bias_value
    losses = -jax.nn.log_sigmoid(label_signs * logits)
    pair_grads = -label_signs * jax.nn.sigmoid(-label_signs * logits)
    return (jnp.sum(losses), jnp.sum(pair_grads * logit_scale * cosine), jnp.sum(pair_grads), pair_grads.astype(jnp.bfloat16))

def reference(image_feats, text_feats, image_proj, text_proj, log_scale, logit_bias):
    image_unit, image_norm = normalize(image_feats, image_proj)
    text_unit, text_norm = normalize(text_feats, text_proj)
    image_half = image_unit.astype(jnp.bfloat16)
    text_half = text_unit.astype(jnp.bfloat16)
    logit_scale = jnp.exp(log_scale[0])
    bias_value = logit_bias[0]
    block_rows = math.gcd(BATCH, 512)
    columns = jnp.arange(BATCH, dtype=jnp.int32)

    def score_block(running, offset):
        text_grad, loss_sum, scale_sum, bias_sum = running
        row_block = lax.dynamic_slice_in_dim(image_half, offset, block_rows, 0)
        cosine = jnp.dot(row_block, text_half.T, preferred_element_type=jnp.float32)
        row_ids = offset + jnp.arange(block_rows, dtype=jnp.int32)
        label_signs = jnp.where(row_ids[:, None] == columns[None, :], 1.0, -1.0).astype(jnp.float32)
        loss_part, scale_part, bias_part, half_grads = pair_terms(cosine, label_signs, logit_scale, bias_value)
        image_grad = logit_scale * jnp.dot(half_grads, text_half, preferred_element_type=jnp.float32)
        text_grad = text_grad + logit_scale * jnp.dot(half_grads.T, row_block, preferred_element_type=jnp.float32)
        return ((text_grad, loss_sum + loss_part, scale_sum + scale_part, bias_sum + bias_part), image_grad)
    offsets = jnp.arange(BATCH // block_rows, dtype=jnp.int32) * block_rows
    starting = (jnp.zeros((BATCH, WIDTH), jnp.float32), jnp.zeros((), jnp.float32), jnp.zeros((), jnp.float32), jnp.zeros((), jnp.float32))
    finished, image_blocks = lax.scan(score_block, starting, offsets)
    text_grad, loss_sum, scale_sum, bias_sum = finished
    image_grad = image_blocks.reshape(BATCH, WIDTH)
    image_dy = unnormalize(image_unit, image_norm, image_grad)
    text_dy = unnormalize(text_unit, text_norm, text_grad)
    image_proj_grad = jnp.dot(image_feats.T, image_dy, preferred_element_type=jnp.float32)
    text_proj_grad = jnp.dot(text_feats.T, text_dy, preferred_element_type=jnp.float32)
    return ((loss_sum / BATCH).reshape(1), image_proj_grad, text_proj_grad, (scale_sum / BATCH).reshape(1), (bias_sum / BATCH).reshape(1))
```

```python
import functools

import jax
import jax.numpy as jnp
from jax import lax
from jax.experimental import pallas as pl
from jax.experimental.pallas import tpu as pltpu
from jax.sharding import PartitionSpec as P

MESH = pl.DeviceIdType.MESH
BF16, F32 = jnp.bfloat16, jnp.float32
WIDTH = 1152
OWN = 128
UNIT = 2 * OWN
ROWS = 8 * UNIT
TILE = 512
PART = WIDTH // 3
LOG2E = 1.4426950408889634

UNITS = {(0, 0): 0, (1, 0): 1, (0, 3): 2, (0, 1): 3, (1, 3): 4, (1, 1): 5, (0, 2): 6, (1, 2): 7}
RING_UP = [((0, 0, 0), (0, 3, 0)), ((0, 0, 1), (0, 3, 1)), ((1, 0, 1), (1, 3, 1)), ((0, 3, 1), (0, 2, 1)), ((1, 3, 1), (1, 2, 1))]
RING_DOWN = [((0, 0, 0), (0, 1, 0)), ((0, 0, 1), (0, 1, 1)), ((0, 1, 0), (0, 2, 0)), ((1, 0, 1), (1, 1, 1)), ((1, 1, 0), (1, 2, 0))]
ACROSS = [((0, 0, 0), (1, 0, 0)), ((0, 0, 1), (1, 0, 1)), ((0, 1, 0), (1, 1, 0)), ((0, 3, 0), (1, 3, 0))]
ORDERS = [(0, 1, 2), (1, 2, 0), (2, 0, 1)]


def device(x, y, z, core):
    x, y, z = lax.rem(x, 4), lax.rem(y, 4), lax.rem(z, 4)
    return (lax.rem(z, 2) * 16 + x * 4 + y, lax.div(z, 2) * 2 + core)


def natural_row(x, y, z):
    return 18 * (((z % 2) * 16 + x * 4 + y) * 2 + z // 2)


def fold(v):
    return v[0:8] + v[8:16] + v[16:24] + v[24:32]


def kernel(
    log_scale, logit_bias, image_feats, text_feats, image_proj, text_proj,
    loss_out, image_out, text_out, scale_out, bias_out,
    feats, feats_t, unit, unit_low, other, pairs, pairs_t, proj, inv_norm, wide, perm, sums,
    first_a, first_b, first_c, into_a, into_b, into_c, part_sum, second_out, second_in, third_out, third_own, third_in,
    scalars, last, last_in,
    local_sem, gather_send, gather_recv, unit_send, unit_recv, tile_send, tile_recv,
    first_send, first_recv, second_send, second_recv, third_send, third_recv, scalar_send, scalar_recv, last_sem,
):
    dp, mp = lax.axis_index("dp"), lax.axis_index("mp")
    core = lax.rem(mp, 2)
    x = lax.rem(lax.div(dp, 4), 4)
    y = lax.rem(dp, 4)
    z = lax.div(mp, 2) * 2 + lax.div(dp, 16)
    pos = (x, y, z)
    is_image = core == 0
    sibling = (dp, mp + 1 - 2 * core)

    def along(axis, step):
        moved = [x, y, z]
        moved[axis] = moved[axis] + step
        return device(*moved, core)

    def ring(step):
        return device(jnp.where(is_image, x, x + step), y, jnp.where(is_image, z + step, z), core)

    even = lax.rem(y, 2) == 0
    across = device(x, jnp.where(is_image == even, y + 1, y + 3), z, core)

    def remote(src, dst, send, recv, to):
        return pltpu.make_async_remote_copy(
            src_ref=src, dst_ref=dst, send_sem=send, recv_sem=recv, device_id=to, device_id_type=MESH
        )

    def slot(key):
        dy, dr, half = key
        side = core if half == 0 else 1 - core
        return pl.ds(pl.multiple_of(UNITS[(dy, dr)] * UNIT + side * OWN, OWN), OWN)

    def arrival(key):
        return gather_recv.at[UNITS[key[:2]] * 2 + key[2]]

    own = slot((0, 0, 0))
    own_copy = pltpu.make_async_copy(image_feats, feats.at[own], local_sem.at[0])
    proj_copy = pltpu.make_async_copy(image_proj, proj, local_sem.at[1])

    @pl.when(is_image)
    def _():
        own_copy.start()
        proj_copy.start()

    @pl.when(jnp.logical_not(is_image))
    def _():
        pltpu.make_async_copy(text_feats, feats.at[own], local_sem.at[0]).start()
        pltpu.make_async_copy(text_proj, proj, local_sem.at[1]).start()

    barrier = pltpu.get_barrier_semaphore()
    partners = [along(axis, step) for axis in range(3) for step in (1, 2, 3)] + [sibling]
    for partner in partners:
        pl.semaphore_signal(barrier, inc=1, device_id=partner, device_id_type=MESH)
    pl.semaphore_wait(barrier, len(partners))

    def cross(src):
        return remote(src, feats.at[own], gather_send.at[14], gather_recv.at[1], sibling)

    @pl.when(is_image)
    def _():
        cross(text_feats).start()

    @pl.when(jnp.logical_not(is_image))
    def _():
        cross(image_feats).start()

    own_copy.wait()

    sends = {}
    for index, (path, to) in enumerate(((RING_UP, ring(1)), (RING_DOWN, ring(3)), (ACROSS, across))):
        for step, (source, target) in enumerate(path):
            sends[(index, step)] = remote(
                feats.at[slot(source)], feats.at[slot(target)], gather_send.at[index * 5 + step], arrival(target), to
            )

    def arrived(*key):
        remote(feats.at[slot(key)], feats.at[slot(key)], gather_send.at[0], arrival(key), sibling).wait_recv()

    for index in range(3):
        sends[(index, 0)].start()
    arrived(0, 0, 1)
    for index in range(3):
        sends[(index, 1)].start()
    proj_copy.wait()

    def unit_copy(index):
        rows = pl.ds(pl.multiple_of(index * UNIT, UNIT), UNIT)
        return remote(unit.at[rows], other.at[rows], unit_send.at[index], unit_recv.at[index], sibling)

    def project(index, carry):
        rows = pl.ds(pl.multiple_of(index * UNIT, UNIT), UNIT)
        wide[pl.ds(0, UNIT), :] = jnp.dot(feats[rows, :], proj[...], preferred_element_type=F32)

        def chunk(i, c):
            here = pl.ds(pl.multiple_of(i * 32, 32), 32)
            there = pl.ds(pl.multiple_of(index * UNIT + i * 32, 32), 32)
            raw = wide[here, :]
            inv = 1.0 / jnp.sqrt(jnp.sum(raw * raw, axis=1, keepdims=True) + 1e-06)
            value = raw * inv
            half = value.astype(BF16)
            unit[there, :] = half
            unit_low[there, :] = (value - half.astype(F32)).astype(BF16)
            inv_norm[there, :] = inv
            return c

        lax.fori_loop(0, UNIT // 32, chunk, 0)
        unit_copy(index).start()
        feats_t[:, rows] = feats[rows, :].T
        return carry

    scale = jnp.exp(jnp.full((1, TILE), log_scale[0], F32))
    slope = scale * LOG2E
    offset = jnp.full((1, TILE), logit_bias[0], F32) * LOG2E

    def tile_copy(t, a, b):
        return remote(
            pairs_t.at[t],
            pairs.at[pl.ds(pl.multiple_of(b * TILE, TILE), TILE), pl.ds(pl.multiple_of(a * TILE, TILE), TILE)],
            tile_send.at[t], tile_recv.at[t], sibling,
        )

    def tile_place(t):
        a = jnp.where(t < 4, lax.rem(t, 2), 2 + lax.div(t - 4, 2))
        b = lax.rem(a + core, 2) + jnp.where(t < 2, 0, jnp.where(t < 4, 2, 2 * lax.rem(t, 2)))
        return a, b

    def tile(t, carry):
        a, b = tile_place(t)
        rows = pl.ds(pl.multiple_of(a * TILE, TILE), TILE)
        cols = pl.ds(pl.multiple_of(b * TILE, TILE), TILE)
        wide[pl.ds(0, TILE), pl.ds(0, TILE)] = lax.dot_general(
            unit[rows, :], other[cols, :], (((1,), (1,)), ((), ())), preferred_element_type=F32
        )

        def run(diagonal):
            def chunk(i, acc):
                here = pl.ds(pl.multiple_of(i * 32, 32), 32)
                cosine = wide[here, pl.ds(0, TILE)]
                arg = cosine * slope + offset
                if diagonal:
                    row = i * 32 + lax.broadcasted_iota(jnp.int32, (32, TILE), 0)
                    col = lax.broadcasted_iota(jnp.int32, (32, TILE), 1)
                    sign = jnp.where((row == col) & (col < UNIT), -1.0, 1.0).astype(F32)
                    arg = arg * sign
                up = jnp.exp2(arg)
                whole = 1.0 + up
                inv = pl.reciprocal(whole, approx=True)
                inv = inv * (2.0 - whole * inv)
                grad = up * inv
                loss = jnp.log(whole) + (up - (whole - 1.0)) * inv
                if diagonal:
                    grad = grad * sign
                pairs[pl.ds(pl.multiple_of(a * TILE + i * 32, 32), 32), cols] = grad.astype(BF16)
                return acc[0] + fold(loss), acc[1] + fold(grad * cosine), acc[2] + fold(grad)

            zero = jnp.zeros((8, TILE), F32)
            acc = lax.fori_loop(0, TILE // 32, chunk, (zero, zero, zero))
            for k in range(3):
                sums[k] += acc[k]

        on_diagonal = jnp.logical_and(is_image, t == 0)
        pl.when(on_diagonal)(lambda: run(True))
        pl.when(jnp.logical_not(on_diagonal))(lambda: run(False))
        pairs_t[t] = pairs[rows, cols].T
        tile_copy(t, a, b).start()
        return carry

    sums[...] = jnp.zeros_like(sums)
    project(0, 0)
    arrived(0, 1, 0)
    sends[(1, 2)].start()
    sends[(2, 2)].start()
    arrived(0, 3, 0)
    sends[(2, 3)].start()
    arrived(1, 0, 0)
    arrived(1, 0, 1)
    sends[(0, 2)].start()
    sends[(1, 3)].start()
    arrived(0, 3, 1)
    sends[(0, 3)].start()
    arrived(0, 1, 1)
    lax.fori_loop(1, 4, project, 0)
    arrived(1, 3, 1)
    sends[(0, 4)].start()
    arrived(1, 1, 0)
    sends[(1, 4)].start()
    for index in range(4):
        unit_copy(index).wait_recv()
    lax.fori_loop(0, 2, tile, 0)
    for key in ((0, 2, 0), (0, 2, 1), (1, 1, 1), (1, 3, 0)):
        arrived(*key)
    lax.fori_loop(4, 7, project, 0)
    arrived(1, 2, 0)
    arrived(1, 2, 1)
    project(7, 0)
    for index in range(4, 8):
        unit_copy(index).wait_recv()
    lax.fori_loop(2, 8, tile, 0)

    def scalar_copies(stage):
        if stage == 3:
            return [remote(scalars.at[3, core], scalars.at[3, core], scalar_send.at[9], scalar_recv.at[9], sibling)]
        return [
            remote(
                scalars.at[stage, pos[stage]], scalars.at[stage, pos[stage]],
                scalar_send.at[stage * 3 + step - 1], scalar_recv.at[stage * 3 + step - 1], along(stage, step),
            )
            for step in (1, 2, 3)
        ]

    def scalar_start(stage, value):
        scalars[stage, pos[stage] if stage < 3 else core] = value
        for copy in scalar_copies(stage):
            copy.start()

    def scalar_finish(stage):
        for copy in scalar_copies(stage):
            copy.wait()
        if stage == 3:
            return scalars[3, 0] + scalars[3, 1]
        return (scalars[stage, 0] + scalars[stage, 1]) + (scalars[stage, 2] + scalars[stage, 3])

    lanes = [sums[k][:, 0:128] + sums[k][:, 128:256] + (sums[k][:, 256:384] + sums[k][:, 384:512]) for k in range(3)]
    scalar_start(0, jnp.concatenate(lanes, axis=0))

    for copy in sends.values():
        copy.wait_send()
    cross(text_feats).wait_send()
    for t in range(8):
        tile_copy(t, 0, 0).wait_recv()

    scale_row = jnp.exp(jnp.full((1, 1), log_scale[0], F32))

    def backward(a, carry):
        rows = pl.ds(pl.multiple_of(a * TILE, TILE), TILE)
        wide[pl.ds(0, TILE), :] = jnp.dot(pairs[rows, :], other[...], preferred_element_type=F32)

        def chunk(i, c):
            here = pl.ds(pl.multiple_of(i * 32, 32), 32)
            there = pl.ds(pl.multiple_of(a * TILE + i * 32, 32), 32)
            grad = wide[here, :]
            value = unit[there, :].astype(F32) + unit_low[there, :].astype(F32)
            inner = jnp.sum(value * grad, axis=1, keepdims=True)
            feats[there, :] = ((grad - value * inner) * (inv_norm[there, :] * scale_row)).astype(BF16)
            return c

        lax.fori_loop(0, TILE // 32, chunk, 0)
        return carry

    lax.fori_loop(0, 4, backward, 0)
    scalar_start(1, scalar_finish(0))

    def weight_tile(n, carry):
        cols = pl.ds(pl.multiple_of(n * 256, 256), 256)
        wide[:, cols] = jnp.dot(feats_t[...], feats[:, cols], preferred_element_type=F32)
        return carry

    up = 1 - 2 * core

    def first_copies(p):
        axis = ORDERS[p][0]
        ahead, behind = along(axis, lax.rem(4 + up, 4)), along(axis, lax.rem(4 - up, 4))
        return (
            remote(first_a.at[p], into_a.at[p], first_send.at[p, 0], first_recv.at[p, 0], ahead),
            remote(first_b.at[p], into_b.at[p], first_send.at[p, 1], first_recv.at[p, 1], behind),
            remote(first_c.at[p], into_c.at[p], first_send.at[p, 2], first_recv.at[p, 2], ahead),
        )

    def block(p, step):
        k = lax.rem(pos[ORDERS[p][0]] + 4 + step, 4)
        return pl.ds(pl.multiple_of(k * 288, 288), 288), pl.ds(p * PART, PART)

    def first_start(p):
        columns = pl.ds(p * PART, PART)
        for k1 in range(4):
            for k2 in range(4):
                for k3 in range(4):
                    place = [0, 0, 0]
                    for axis, k in zip(ORDERS[p], (k1, k2, k3)):
                        place[axis] = k
                    perm[pl.ds(k1 * 288 + k2 * 72 + k3 * 18, 18), columns] = wide[pl.ds(natural_row(*place), 18), columns]
        first_a[p] = perm[block(p, 2)].astype(BF16)
        first_b[p] = perm[block(p, -up)].astype(BF16)
        copies = first_copies(p)
        copies[0].start()
        copies[1].start()

    def first_forward(p):
        copies = first_copies(p)
        copies[0].wait_recv()
        first_c[p] = (perm[block(p, up)] + into_a[p].astype(F32)).astype(BF16)
        copies[2].start()

    def second_copies(p):
        return [
            remote(second_out.at[p, step - 1], second_in.at[p, step - 1], second_send.at[p, step - 1],
                   second_recv.at[p, step - 1], along(ORDERS[p][1], step))
            for step in (1, 2, 3)
        ]

    def second_rows(p, step):
        return pl.ds(pl.multiple_of(lax.rem(pos[ORDERS[p][1]] + step, 4) * 72, 8), 72)

    def second_start(p):
        copies = first_copies(p)
        copies[1].wait_recv()
        copies[2].wait_recv()
        part_sum[p] = perm[block(p, 0)] + into_b[p].astype(F32) + into_c[p].astype(F32)
        for step, copy in zip((1, 2, 3), second_copies(p)):
            second_out[p, step - 1, pl.ds(0, 72), :] = part_sum[p, second_rows(p, step), :].astype(BF16)
            copy.start()

    def third_copies(p):
        at = pos[ORDERS[p][2]]
        return [
            remote(third_out.at[p, lax.rem(at + step, 4)], third_in.at[p, step - 1], third_send.at[p, step - 1],
                   third_recv.at[p, step - 1], along(ORDERS[p][2], step))
            for step in (1, 2, 3)
        ]

    def third_start(p):
        total = part_sum[p, second_rows(p, 0), :]
        for step, copy in zip((1, 2, 3), second_copies(p)):
            copy.wait_recv()
            total += second_in[p, step - 1, pl.ds(0, 72), :].astype(F32)
        part_sum[p, pl.ds(0, 72), :] = total
        for k in range(4):
            piece = part_sum[p, pl.ds(18 * k, 18), :]
            third_own[p, k, pl.ds(0, 18), :] = piece
            third_out[p, k, pl.ds(0, 18), :] = piece.astype(BF16)
        for copy in third_copies(p):
            copy.start()

    def third_finish(p):
        total = third_own[p, pos[ORDERS[p][2]], pl.ds(0, 18), :]
        for step, copy in zip((1, 2, 3), third_copies(p)):
            copy.wait_recv()
            total += third_in[p, step - 1, pl.ds(0, 18), :].astype(F32)
        third_own[p, 0, pl.ds(0, 18), :] = total
        columns = pl.ds(p * PART, PART)
        for h in range(2):
            last[h, pl.ds(0, 9), columns] = third_own[p, 0, pl.ds(9 * h, 9), :]

    lax.fori_loop(0, 2, weight_tile, 0)
    first_start(0)
    lax.fori_loop(2, 3, weight_tile, 0)
    first_start(1)
    lax.fori_loop(3, 4, weight_tile, 0)
    first_forward(0)
    wide[:, pl.ds(1024, 128)] = jnp.dot(feats_t[...], feats[:, pl.ds(1024, 128)], preferred_element_type=F32)
    first_start(2)
    first_forward(1)
    scalar_start(2, scalar_finish(1))
    second_start(0)
    first_forward(2)
    second_start(1)
    scalar_start(3, scalar_finish(2))
    third_start(0)
    second_start(2)
    third_start(1)
    totals = scalar_finish(3)
    third_finish(0)
    third_start(2)
    third_finish(1)
    batch = 1.0 / 16384.0
    loss_out[0] = jnp.sum(totals[0:8]) * batch
    scale_out[0] = jnp.sum(totals[8:16] * jnp.exp(jnp.full((8, 128), log_scale[0], F32))) * batch
    bias_out[0] = jnp.sum(totals[16:24]) * batch
    third_finish(2)

    exchange = remote(last.at[1 - core], last_in, last_sem.at[0], last_sem.at[1], sibling)
    exchange.start()
    for p in range(3):
        for copy in first_copies(p) + tuple(second_copies(p)) + tuple(third_copies(p)):
            copy.wait_send()
    for index in range(8):
        unit_copy(index).wait_send()
        tile_copy(index, 0, 0).wait_send()
    exchange.wait()
    rows = pl.ds(0, 9)

    @pl.when(is_image)
    def _():
        image_out[...] = last[0, rows, :]
        text_out[...] = last_in[rows, :]

    @pl.when(jnp.logical_not(is_image))
    def _():
        image_out[...] = last_in[rows, :]
        text_out[...] = last[1, rows, :]


def per_device(image_feats, text_feats, image_proj, text_proj, log_scale, logit_bias):
    smem = pl.BlockSpec(memory_space=pltpu.SMEM)
    vmem = pl.BlockSpec(memory_space=pltpu.VMEM)
    hbm = pl.BlockSpec(memory_space=pl.ANY)
    dma, buffer = pltpu.SemaphoreType.DMA, pltpu.VMEM
    one = jax.ShapeDtypeStruct((1,), F32)
    rows = jax.ShapeDtypeStruct((9, WIDTH), F32)
    loss, image_grad, text_grad, scale_grad, bias_grad = pl.pallas_call(
        kernel,
        out_shape=(one, rows, rows, one, one),
        in_specs=[smem, smem, hbm, hbm, hbm, hbm],
        out_specs=(smem, vmem, vmem, smem, smem),
        scratch_shapes=[
            buffer((ROWS, WIDTH), BF16),
            buffer((WIDTH, ROWS), BF16),
            buffer((ROWS, WIDTH), BF16),
            buffer((ROWS, WIDTH), BF16),
            buffer((ROWS, WIDTH), BF16),
            buffer((ROWS, ROWS), BF16),
            buffer((8, TILE, TILE), BF16),
            buffer((WIDTH, WIDTH), BF16),
            buffer((ROWS, 1), F32),
            buffer((WIDTH, WIDTH), F32),
            buffer((WIDTH, WIDTH), F32),
            buffer((3, 8, TILE), F32),
            *[buffer((3, 288, PART), BF16) for _ in range(6)],
            buffer((3, 288, PART), F32),
            buffer((3, 3, 80, PART), BF16),
            buffer((3, 3, 80, PART), BF16),
            buffer((3, 4, 32, PART), BF16),
            buffer((3, 4, 24, PART), F32),
            buffer((3, 3, 32, PART), BF16),
            buffer((4, 4, 24, 128), F32),
            buffer((2, 16, WIDTH), F32),
            buffer((16, WIDTH), F32),
            dma((2,)),
            dma((15,)), dma((16,)),
            dma((8,)), dma((8,)),
            dma((8,)), dma((8,)),
            dma((3, 3)), dma((3, 3)),
            dma((3, 3)), dma((3, 3)),
            dma((3, 3)), dma((3, 3)),
            dma((10,)), dma((10,)),
            dma((2,)),
        ],
        compiler_params=pltpu.CompilerParams(collective_id=0, has_side_effects=True, vmem_limit_bytes=62 * 2**20),
        name="sigmoid_loss",
    )(log_scale, logit_bias, image_feats, text_feats, image_proj, text_proj)
    return loss, image_grad, text_grad, scale_grad, bias_grad


def solution(mesh):
    return jax.shard_map(
        per_device,
        mesh=mesh,
        in_specs=(P(("dp", "mp"), None), P(("dp", "mp"), None), P(), P(), P(), P()),
        out_specs=(P(), P(("dp", "mp"), None), P(("dp", "mp"), None), P(), P()),
        check_vma=False,
    )
```

```python
import functools

import jax
import jax.numpy as jnp
from jax import lax
from jax.experimental import pallas as pl
from jax.experimental.pallas import tpu as pltpu
from jax.sharding import PartitionSpec as P

MESH = pl.DeviceIdType.MESH
BF16, F32 = jnp.bfloat16, jnp.float32
WIDTH = 1152
OWN = 128
UNIT = 2 * OWN
ROWS = 8 * UNIT
TILE = 512
PART = 128
THIRD = 3 * PART
STEP = 16
LOG2E = 1.4426950408889634

UNITS = {(0, 0): 0, (1, 0): 1, (0, 3): 2, (0, 1): 3, (1, 3): 4, (1, 1): 5, (0, 2): 6, (1, 2): 7}
RING_UP = [((0, 0, 0), (0, 3, 0)), ((0, 0, 1), (0, 3, 1)), ((1, 0, 1), (1, 3, 1)), ((0, 3, 1), (0, 2, 1)), ((1, 3, 1), (1, 2, 1))]
RING_DOWN = [((0, 0, 0), (0, 1, 0)), ((0, 0, 1), (0, 1, 1)), ((0, 1, 0), (0, 2, 0)), ((1, 0, 1), (1, 1, 1)), ((1, 1, 0), (1, 2, 0))]
ACROSS = [((0, 0, 0), (1, 0, 0)), ((0, 0, 1), (1, 0, 1)), ((0, 1, 0), (1, 1, 0)), ((0, 3, 0), (1, 3, 0))]
ORDERS = [(0, 1, 2), (1, 2, 0), (2, 0, 1)]


def device(x, y, z, core):
    x, y, z = lax.rem(x, 4), lax.rem(y, 4), lax.rem(z, 4)
    return (lax.rem(z, 2) * 16 + x * 4 + y, lax.div(z, 2) * 2 + core)


def natural_row(x, y, z):
    return 18 * (((z % 2) * 16 + x * 4 + y) * 2 + z // 2)


def fold(v):
    return v[0:8] + v[8:16]


def kernel(
    log_scale, logit_bias, image_feats, text_feats, image_proj, text_proj,
    loss_out, image_out, text_out, scale_out, bias_out,
    feats, feats_t, unit, unit_low, other, pairs, pairs_t, proj, inv_norm, wide, perm, sums,
    first_a, first_b, into_a, into_b, into_c, part_sum, second_out, second_in, third_own, third_in,
    scalars, last, last_in,
    local_sem, gather_send, gather_recv, unit_send, unit_recv, tile_send, tile_recv,
    first_send, first_recv, second_send, second_recv, third_send, third_recv, scalar_send, scalar_recv, last_sem,
):
    dp, mp = lax.axis_index("dp"), lax.axis_index("mp")
    core = lax.rem(mp, 2)
    x = lax.rem(lax.div(dp, 4), 4)
    y = lax.rem(dp, 4)
    z = lax.div(mp, 2) * 2 + lax.div(dp, 16)
    pos = (x, y, z)
    is_image = core == 0
    sibling = (dp, mp + 1 - 2 * core)

    def along(axis, step):
        moved = [x, y, z]
        moved[axis] = moved[axis] + step
        return device(*moved, core)

    def ring(step):
        return device(jnp.where(is_image, x, x + step), y, jnp.where(is_image, z + step, z), core)

    even = lax.rem(y, 2) == 0
    across = device(x, jnp.where(is_image == even, y + 1, y + 3), z, core)

    def remote(src, dst, send, recv, to):
        return pltpu.make_async_remote_copy(
            src_ref=src, dst_ref=dst, send_sem=send, recv_sem=recv, device_id=to, device_id_type=MESH
        )

    def slot(key):
        dy, dr, half = key
        side = core if half == 0 else 1 - core
        return pl.ds(pl.multiple_of(UNITS[(dy, dr)] * UNIT + side * OWN, OWN), OWN)

    def arrival(key):
        return gather_recv.at[UNITS[key[:2]] * 2 + key[2]]

    own = slot((0, 0, 0))
    own_copy = pltpu.make_async_copy(image_feats, feats.at[own], local_sem.at[0])
    proj_copy = pltpu.make_async_copy(image_proj, proj, local_sem.at[1])

    @pl.when(is_image)
    def _():
        own_copy.start()
        proj_copy.start()

    @pl.when(jnp.logical_not(is_image))
    def _():
        pltpu.make_async_copy(text_feats, feats.at[own], local_sem.at[0]).start()
        pltpu.make_async_copy(text_proj, proj, local_sem.at[1]).start()

    barrier = pltpu.get_barrier_semaphore()
    partners = [along(axis, step) for axis in range(3) for step in (1, 2, 3)] + [sibling]
    for partner in partners:
        pl.semaphore_signal(barrier, inc=1, device_id=partner, device_id_type=MESH)
    pl.semaphore_wait(barrier, len(partners))

    def cross(src):
        return remote(src, feats.at[own], gather_send.at[14], gather_recv.at[1], sibling)

    @pl.when(is_image)
    def _():
        cross(text_feats).start()

    @pl.when(jnp.logical_not(is_image))
    def _():
        cross(image_feats).start()

    own_copy.wait()

    sends = {}
    for index, (path, to) in enumerate(((RING_UP, ring(1)), (RING_DOWN, ring(3)), (ACROSS, across))):
        for step, (source, target) in enumerate(path):
            sends[(index, step)] = remote(
                feats.at[slot(source)], feats.at[slot(target)], gather_send.at[index * 5 + step], arrival(target), to
            )

    def arrived(*key):
        remote(feats.at[slot(key)], feats.at[slot(key)], gather_send.at[0], arrival(key), sibling).wait_recv()

    for index in range(3):
        sends[(index, 0)].start()
    arrived(0, 0, 1)
    for index in range(3):
        sends[(index, 1)].start()
    proj_copy.wait()

    def unit_copy(index):
        rows = pl.ds(pl.multiple_of(index * UNIT, UNIT), UNIT)
        return remote(unit.at[rows], other.at[rows], unit_send.at[index], unit_recv.at[index], sibling)

    def project(index, buffer):
        rows = pl.ds(pl.multiple_of(index * UNIT, UNIT), UNIT)
        buffer[pl.ds(0, UNIT), :] = jnp.dot(feats[rows, :], proj[...], preferred_element_type=F32)
        feats_t[:, rows] = feats[rows, :].T

    def normalize(index, buffer):
        for i in range(UNIT // STEP):
            there = pl.ds(pl.multiple_of(index * UNIT + i * STEP, STEP), STEP)
            raw = buffer[pl.ds(i * STEP, STEP), :]
            inv = 1.0 / jnp.sqrt(jnp.sum(raw * raw, axis=1, keepdims=True) + 1e-06)
            value = raw * inv
            half = value.astype(BF16)
            unit[there, :] = half
            unit_low[there, :] = (value - half.astype(F32)).astype(BF16)
            inv_norm[there, :] = inv

    def three_units(first):
        project(first, wide)
        project(first + 1, perm)
        normalize(first, wide)
        unit_copy(first).start()
        project(first + 2, wide)
        normalize(first + 1, perm)
        unit_copy(first + 1).start()
        normalize(first + 2, wide)
        unit_copy(first + 2).start()

    scale = jnp.exp(jnp.full((1, TILE), log_scale[0], F32))
    slope = scale * LOG2E
    offset = jnp.full((1, TILE), logit_bias[0], F32) * LOG2E

    def tile_copy(t, a, b):
        return remote(
            pairs_t.at[t],
            pairs.at[pl.ds(pl.multiple_of(b * TILE, TILE), TILE), pl.ds(pl.multiple_of(a * TILE, TILE), TILE)],
            tile_send.at[t], tile_recv.at[t], sibling,
        )

    def tile_place(t):
        a = jnp.where(t < 4, lax.rem(t, 2), 2 + lax.div(t - 4, 2))
        b = lax.rem(a + core, 2) + jnp.where(t < 2, 0, jnp.where(t < 4, 2, 2 * lax.rem(t, 2)))
        return a, b

    def cosines(t, buffer):
        a, b = tile_place(t)
        rows = pl.ds(pl.multiple_of(a * TILE, TILE), TILE)
        cols = pl.ds(pl.multiple_of(b * TILE, TILE), TILE)
        buffer[pl.ds(0, TILE), pl.ds(0, TILE)] = lax.dot_general(
            unit[rows, :], other[cols, :], (((1,), (1,)), ((), ())), preferred_element_type=F32
        )

    def pair_terms(t, buffer, diagonal):
        a, b = tile_place(t)
        cols = pl.ds(pl.multiple_of(b * TILE, TILE), TILE)
        acc = [jnp.zeros((8, TILE), F32) for _ in range(3)]
        for i in range(TILE // STEP):
            cosine = buffer[pl.ds(i * STEP, STEP), pl.ds(0, TILE)]
            arg = cosine * slope + offset
            masked = diagonal and i < UNIT // STEP
            if masked:
                row = i * STEP + lax.broadcasted_iota(jnp.int32, (STEP, TILE), 0)
                col = lax.broadcasted_iota(jnp.int32, (STEP, TILE), 1) + core * ROWS
                sign = jnp.where(row == col, -1.0, 1.0).astype(F32)
                arg = arg * sign
            up = jnp.exp2(arg)
            whole = 1.0 + up
            inv = pl.reciprocal(whole, approx=True)
            inv = inv * (2.0 - whole * inv)
            grad = up * inv
            loss = jnp.log(whole) + (up - (whole - 1.0)) * inv
            if masked:
                grad = grad * sign
            pairs[pl.ds(pl.multiple_of(a * TILE + i * STEP, STEP), STEP), cols] = grad.astype(BF16)
            acc = [acc[0] + fold(loss), acc[1] + fold(grad * cosine), acc[2] + fold(grad)]
        for k in range(3):
            sums[k] += acc[k]

    def hand_over(t):
        a, b = tile_place(t)
        rows = pl.ds(pl.multiple_of(a * TILE, TILE), TILE)
        cols = pl.ds(pl.multiple_of(b * TILE, TILE), TILE)
        pairs_t[t] = pairs[rows, cols].T
        tile_copy(t, a, b).start()

    def two_tiles(i, carry):
        t = 2 * i
        cosines(t + 1, perm)
        pair_terms(t, wide, False)
        hand_over(t)
        cosines(t + 2, wide)
        pair_terms(t + 1, perm, False)
        hand_over(t + 1)
        return carry

    sums[...] = jnp.zeros_like(sums)
    project(0, wide)
    normalize(0, wide)
    unit_copy(0).start()
    arrived(0, 1, 0)
    sends[(1, 2)].start()
    sends[(2, 2)].start()
    arrived(0, 3, 0)
    sends[(2, 3)].start()
    arrived(1, 0, 0)
    arrived(1, 0, 1)
    sends[(0, 2)].start()
    sends[(1, 3)].start()
    arrived(0, 3, 1)
    sends[(0, 3)].start()
    arrived(0, 1, 1)
    three_units(1)
    arrived(1, 3, 1)
    sends[(0, 4)].start()
    arrived(1, 1, 0)
    sends[(1, 4)].start()
    for index in range(4):
        unit_copy(index).wait_recv()
    cosines(0, wide)
    cosines(1, perm)
    pair_terms(0, wide, True)
    hand_over(0)
    pair_terms(1, perm, False)
    hand_over(1)
    for key in ((0, 2, 0), (0, 2, 1), (1, 1, 1), (1, 3, 0)):
        arrived(*key)
    three_units(4)
    arrived(1, 2, 0)
    arrived(1, 2, 1)
    project(7, wide)
    normalize(7, wide)
    unit_copy(7).start()
    for index in range(4, 8):
        unit_copy(index).wait_recv()
    cosines(2, wide)
    lax.fori_loop(1, 3, two_tiles, 0)
    cosines(7, perm)
    pair_terms(6, wide, False)
    hand_over(6)
    pair_terms(7, perm, False)
    hand_over(7)

    def scalar_copies(stage):
        if stage == 3:
            return [remote(scalars.at[3, core], scalars.at[3, core], scalar_send.at[9], scalar_recv.at[9], sibling)]
        return [
            remote(
                scalars.at[stage, pos[stage]], scalars.at[stage, pos[stage]],
                scalar_send.at[stage * 3 + step - 1], scalar_recv.at[stage * 3 + step - 1], along(stage, step),
            )
            for step in (1, 2, 3)
        ]

    def scalar_start(stage, value):
        scalars[stage, pos[stage] if stage < 3 else core] = value
        for copy in scalar_copies(stage):
            copy.start()

    def scalar_finish(stage):
        for copy in scalar_copies(stage):
            copy.wait()
        if stage == 3:
            return scalars[3, 0] + scalars[3, 1]
        return (scalars[stage, 0] + scalars[stage, 1]) + (scalars[stage, 2] + scalars[stage, 3])

    lanes = [sums[k][:, 0:128] + sums[k][:, 128:256] + (sums[k][:, 256:384] + sums[k][:, 384:512]) for k in range(3)]
    scalar_start(0, jnp.concatenate(lanes, axis=0))

    for copy in sends.values():
        copy.wait_send()
    cross(text_feats).wait_send()
    for t in range(8):
        tile_copy(t, 0, 0).wait_recv()

    scale_row = jnp.exp(jnp.full((1, 1), log_scale[0], F32))

    def gradients(a, buffer):
        buffer[pl.ds(0, TILE), :] = jnp.dot(pairs[pl.ds(a * TILE, TILE), :], other[...], preferred_element_type=F32)

    def tangents(a, buffer):
        for i in range(TILE // STEP):
            there = pl.ds(a * TILE + i * STEP, STEP)
            grad = buffer[pl.ds(i * STEP, STEP), :]
            value = unit[there, :].astype(F32) + unit_low[there, :].astype(F32)
            inner = jnp.sum(value * grad, axis=1, keepdims=True)
            feats[there, :] = ((grad - value * inner) * (inv_norm[there, :] * scale_row)).astype(BF16)

    gradients(0, wide)
    for a in range(1, 4):
        gradients(a, (wide, perm)[a % 2])
        tangents(a - 1, (perm, wide)[a % 2])
    tangents(3, perm)
    scalar_start(1, scalar_finish(0))

    def weights(t):
        cols = pl.ds(pl.multiple_of(t * THIRD, PART), THIRD)
        wide[:, cols] = jnp.dot(feats_t[...], feats[:, cols], preferred_element_type=F32)

    up = 1 - 2 * core

    def columns(t, p):
        return pl.ds(pl.multiple_of(t * THIRD + p * PART, PART), PART)

    def first_copies(t, p):
        axis, q = ORDERS[p][0], t * 3 + p
        ahead, behind = along(axis, lax.rem(4 + up, 4)), along(axis, lax.rem(4 - up, 4))
        return (
            remote(first_a.at[q], into_a.at[q], first_send.at[q, 0], first_recv.at[q, 0], ahead),
            remote(first_b.at[q], into_b.at[q], first_send.at[q, 1], first_recv.at[q, 1], behind),
            remote(into_a.at[q], into_c.at[q], first_send.at[q, 2], first_recv.at[q, 2], ahead),
        )

    def block(t, p, step):
        k = lax.rem(pos[ORDERS[p][0]] + 4 + step, 4)
        return pl.ds(pl.multiple_of(k * 288, 288), 288), columns(t, p)

    def first_start(t, p):
        for k1 in range(4):
            for k2 in range(4):
                for k3 in range(4):
                    place = [0, 0, 0]
                    for axis, k in zip(ORDERS[p], (k1, k2, k3)):
                        place[axis] = k
                    perm[pl.ds(k1 * 288 + k2 * 72 + k3 * 18, 18), columns(t, p)] = (
                        wide[pl.ds(natural_row(*place), 18), columns(t, p)])
        q = t * 3 + p
        first_a[q] = perm[block(t, p, 2)].astype(BF16)
        first_b[q] = perm[block(t, p, -up)].astype(BF16)
        copies = first_copies(t, p)
        copies[0].start()
        copies[1].start()

    def first_forward(t, p):
        copies, q = first_copies(t, p), t * 3 + p
        copies[0].wait_recv()
        into_a[q] = (perm[block(t, p, up)] + into_a[q].astype(F32)).astype(BF16)
        copies[2].start()

    def second_copies(t, p):
        q = t * 3 + p
        return [
            remote(second_out.at[q, step - 1], second_in.at[q, step - 1], second_send.at[q, step - 1],
                   second_recv.at[q, step - 1], along(ORDERS[p][1], step))
            for step in (1, 2, 3)
        ]

    def second_rows(p, step):
        return pl.ds(pl.multiple_of(lax.rem(pos[ORDERS[p][1]] + step, 4) * 72, 8), 72)

    def second_start(t, p):
        copies, q = first_copies(t, p), t * 3 + p
        copies[1].wait_recv()
        copies[2].wait_recv()
        part_sum[q] = perm[block(t, p, 0)] + into_b[q].astype(F32) + into_c[q].astype(F32)
        for step, copy in zip((1, 2, 3), second_copies(t, p)):
            second_out[q, step - 1, pl.ds(0, 72), :] = part_sum[q, second_rows(p, step), :].astype(BF16)
            copy.start()

    def third_copies(t, p):
        at, q = pos[ORDERS[p][2]], t * 3 + p
        return [
            remote(third_own.at[q, lax.rem(at + step, 4)], third_in.at[q, step - 1], third_send.at[q, step - 1],
                   third_recv.at[q, step - 1], along(ORDERS[p][2], step))
            for step in (1, 2, 3)
        ]

    def third_start(t, p):
        q = t * 3 + p
        total = part_sum[q, second_rows(p, 0), :]
        for step, copy in zip((1, 2, 3), second_copies(t, p)):
            copy.wait_recv()
            total += second_in[q, step - 1, pl.ds(0, 72), :].astype(F32)
        part_sum[q, pl.ds(0, 72), :] = total
        for k in range(4):
            third_own[q, k, pl.ds(0, 18), :] = part_sum[q, pl.ds(18 * k, 18), :]
        for copy in third_copies(t, p):
            copy.start()

    def third_finish(t, p):
        q = t * 3 + p
        total = third_own[q, pos[ORDERS[p][2]], pl.ds(0, 18), :]
        for step, copy in zip((1, 2, 3), third_copies(t, p)):
            copy.wait_recv()
            total += third_in[q, step - 1, pl.ds(0, 18), :]
        part_sum[q, pl.ds(0, 18), :] = total
        for h in range(2):
            last[h, pl.ds(0, 9), columns(t, p)] = part_sum[q, pl.ds(9 * h, 9), :]

    def each(step, t):
        for p in range(3):
            step(t, p)

    def third(t, carry):
        weights(t)

        @pl.when(t > 0)
        def _():
            each(first_forward, t - 1)

        each(first_start, t)

        @pl.when(t > 1)
        def _():
            each(second_start, t - 2)

        return carry

    lax.fori_loop(0, 3, third, 0)
    scalar_start(2, scalar_finish(1))
    each(first_forward, 2)
    each(second_start, 1)
    each(third_start, 0)
    each(second_start, 2)
    scalar_start(3, scalar_finish(2))
    each(third_start, 1)
    each(third_finish, 0)
    each(third_start, 2)
    each(third_finish, 1)
    totals = scalar_finish(3)
    batch = 1.0 / 16384.0
    loss_out[0] = jnp.sum(totals[0:8]) * batch
    scale_out[0] = jnp.sum(totals[8:16] * jnp.exp(jnp.full((8, 128), log_scale[0], F32))) * batch
    bias_out[0] = jnp.sum(totals[16:24]) * batch
    each(third_finish, 2)

    exchange = remote(last.at[1 - core], last_in, last_sem.at[0], last_sem.at[1], sibling)
    exchange.start()

    def sent(t, carry):
        for p in range(3):
            for copy in first_copies(t, p) + tuple(second_copies(t, p)) + tuple(third_copies(t, p)):
                copy.wait_send()
        return carry

    lax.fori_loop(0, 3, sent, 0)
    for index in range(8):
        unit_copy(index).wait_send()
        tile_copy(index, 0, 0).wait_send()
    exchange.wait()
    rows = pl.ds(0, 9)

    @pl.when(is_image)
    def _():
        image_out[...] = last[0, rows, :]
        text_out[...] = last_in[rows, :]

    @pl.when(jnp.logical_not(is_image))
    def _():
        image_out[...] = last_in[rows, :]
        text_out[...] = last[1, rows, :]


def per_device(image_feats, text_feats, image_proj, text_proj, log_scale, logit_bias):
    smem = pl.BlockSpec(memory_space=pltpu.SMEM)
    vmem = pl.BlockSpec(memory_space=pltpu.VMEM)
    hbm = pl.BlockSpec(memory_space=pl.ANY)
    dma, buffer = pltpu.SemaphoreType.DMA, pltpu.VMEM
    one = jax.ShapeDtypeStruct((1,), F32)
    rows = jax.ShapeDtypeStruct((9, WIDTH), F32)
    loss, image_grad, text_grad, scale_grad, bias_grad = pl.pallas_call(
        kernel,
        out_shape=(one, rows, rows, one, one),
        in_specs=[smem, smem, hbm, hbm, hbm, hbm],
        out_specs=(smem, vmem, vmem, smem, smem),
        scratch_shapes=[
            buffer((ROWS, WIDTH), BF16),
            buffer((WIDTH, ROWS), BF16),
            buffer((ROWS, WIDTH), BF16),
            buffer((ROWS, WIDTH), BF16),
            buffer((ROWS, WIDTH), BF16),
            buffer((ROWS, ROWS), BF16),
            buffer((8, TILE, TILE), BF16),
            buffer((WIDTH, WIDTH), BF16),
            buffer((ROWS, 1), F32),
            buffer((WIDTH, WIDTH), F32),
            buffer((WIDTH, WIDTH), F32),
            buffer((3, 8, TILE), F32),
            *[buffer((9, 288, PART), BF16) for _ in range(5)],
            buffer((9, 288, PART), F32),
            buffer((9, 3, 80, PART), BF16),
            buffer((9, 3, 80, PART), BF16),
            buffer((9, 4, 24, PART), F32),
            buffer((9, 3, 24, PART), F32),
            buffer((4, 4, 24, 128), F32),
            buffer((2, 16, WIDTH), F32),
            buffer((16, WIDTH), F32),
            dma((2,)),
            dma((15,)), dma((16,)),
            dma((8,)), dma((8,)),
            dma((8,)), dma((8,)),
            *[dma((9, 3)) for _ in range(6)],
            dma((10,)), dma((10,)),
            dma((2,)),
        ],
        compiler_params=pltpu.CompilerParams(collective_id=0, has_side_effects=True, vmem_limit_bytes=63 * 2**20),
        name="sigmoid_loss",
    )(log_scale, logit_bias, image_feats, text_feats, image_proj, text_proj)
    return loss, image_grad, text_grad, scale_grad, bias_grad


def solution(mesh):
    return jax.shard_map(
        per_device,
        mesh=mesh,
        in_specs=(P(("dp", "mp"), None), P(("dp", "mp"), None), P(), P(), P(), P()),
        out_specs=(P(), P(("dp", "mp"), None), P(("dp", "mp"), None), P(), P()),
        check_vma=False,
    )
```

```python
import functools

import jax
import jax.numpy as jnp
from jax import lax
from jax.experimental import pallas as pl
from jax.experimental.pallas import tpu as pltpu
from jax.sharding import PartitionSpec as P

MESH = pl.DeviceIdType.MESH
BF16, F32 = jnp.bfloat16, jnp.float32
WIDTH = 1152
OWN = 128
UNIT = 2 * OWN
ROWS = 8 * UNIT
TILE = 512
PART = 128
THIRD = 3 * PART
STEP = 16
LOG2E = 1.4426950408889634

UNITS = {(0, 0): 0, (1, 0): 1, (0, 3): 2, (0, 1): 3, (1, 3): 4, (1, 1): 5, (0, 2): 6, (1, 2): 7}
RING_UP = [((0, 0, 0), (0, 3, 0)), ((0, 0, 1), (0, 3, 1)), ((1, 0, 1), (1, 3, 1)), ((0, 3, 1), (0, 2, 1)), ((1, 3, 1), (1, 2, 1))]
RING_DOWN = [((0, 0, 0), (0, 1, 0)), ((0, 0, 1), (0, 1, 1)), ((0, 1, 0), (0, 2, 0)), ((1, 0, 1), (1, 1, 1)), ((1, 1, 0), (1, 2, 0))]
ACROSS = [((0, 0, 0), (1, 0, 0)), ((0, 0, 1), (1, 0, 1)), ((0, 1, 0), (1, 1, 0)), ((0, 3, 0), (1, 3, 0))]
TILES = [
    [(0, 0), (1, 1), (0, 2), (2, 0), (2, 2), (1, 3), (3, 1), (3, 3)],
    [(0, 1), (1, 0), (1, 2), (2, 1), (0, 3), (2, 3), (3, 0), (3, 2)],
]
ORDERS = [(0, 1, 2), (1, 2, 0), (2, 0, 1)]


def device(x, y, z, core):
    x, y, z = lax.rem(x, 4), lax.rem(y, 4), lax.rem(z, 4)
    return (lax.rem(z, 2) * 16 + x * 4 + y, lax.div(z, 2) * 2 + core)


def natural_row(x, y, z):
    return 18 * (((z % 2) * 16 + x * 4 + y) * 2 + z // 2)


def fold(v):
    return v[0:8] + v[8:16]


def kernel(
    log_scale, logit_bias, image_feats, text_feats, image_proj, text_proj,
    out,
    feats, feats_t, unit, unit_low, other, pairs, pairs_t, proj, inv_norm, wide, perm, sums,
    first_a, first_b, into_a, into_b, into_c, part_sum, second_out, second_in, third_own, third_in,
    scalars,
    local_sem, gather_send, gather_recv, unit_send, unit_recv, tile_send, tile_recv,
    first_send, first_recv, second_send, second_recv, third_send, third_recv, scalar_send, scalar_recv,
):
    dp, mp = lax.axis_index("dp"), lax.axis_index("mp")
    core = lax.rem(mp, 2)
    x = lax.rem(lax.div(dp, 4), 4)
    y = lax.rem(dp, 4)
    z = lax.div(mp, 2) * 2 + lax.div(dp, 16)
    pos = (x, y, z)
    is_image = core == 0
    sibling = (dp, mp + 1 - 2 * core)

    def along(axis, step, other_core=False):
        moved = [x, y, z]
        moved[axis] = moved[axis] + step
        return device(*moved, 1 - core if other_core else core)

    def ring(step):
        return device(jnp.where(is_image, x, x + step), y, jnp.where(is_image, z + step, z), core)

    even = lax.rem(y, 2) == 0
    across = device(x, jnp.where(is_image == even, y + 1, y + 3), z, core)

    def remote(src, dst, send, recv, to):
        return pltpu.make_async_remote_copy(
            src_ref=src, dst_ref=dst, send_sem=send, recv_sem=recv, device_id=to, device_id_type=MESH
        )

    def slot(key):
        dy, dr, half = key
        side = core if half == 0 else 1 - core
        return pl.ds(pl.multiple_of(UNITS[(dy, dr)] * UNIT + side * OWN, OWN), OWN)

    def arrival(key):
        return gather_recv.at[UNITS[key[:2]] * 2 + key[2]]

    own = slot((0, 0, 0))
    own_copy = pltpu.make_async_copy(image_feats, feats.at[own], local_sem.at[0])
    proj_copy = pltpu.make_async_copy(image_proj, proj, local_sem.at[1])

    @pl.when(is_image)
    def _():
        own_copy.start()
        proj_copy.start()

    @pl.when(jnp.logical_not(is_image))
    def _():
        pltpu.make_async_copy(text_feats, feats.at[own], local_sem.at[0]).start()
        pltpu.make_async_copy(text_proj, proj, local_sem.at[1]).start()

    barrier = pltpu.get_barrier_semaphore()
    partners = [along(axis, step, flip) for axis in range(3) for step in (1, 2, 3) for flip in (False, True)] + [sibling]
    for partner in partners:
        pl.semaphore_signal(barrier, inc=1, device_id=partner, device_id_type=MESH)
    pl.semaphore_wait(barrier, len(partners))

    def cross(src):
        return remote(src, feats.at[own], gather_send.at[14], gather_recv.at[1], sibling)

    @pl.when(is_image)
    def _():
        cross(text_feats).start()

    @pl.when(jnp.logical_not(is_image))
    def _():
        cross(image_feats).start()

    own_copy.wait()

    sends = {}
    for index, (path, to) in enumerate(((RING_UP, ring(1)), (RING_DOWN, ring(3)), (ACROSS, across))):
        for step, (source, target) in enumerate(path):
            sends[(index, step)] = remote(
                feats.at[slot(source)], feats.at[slot(target)], gather_send.at[index * 5 + step], arrival(target), to
            )

    def arrived(*key):
        remote(feats.at[slot(key)], feats.at[slot(key)], gather_send.at[0], arrival(key), sibling).wait_recv()

    for index in range(3):
        sends[(index, 0)].start()
    arrived(0, 0, 1)
    for index in range(3):
        sends[(index, 1)].start()
    proj_copy.wait()

    def unit_copy(index):
        rows = pl.ds(pl.multiple_of(index * UNIT, UNIT), UNIT)
        return remote(unit.at[rows], other.at[rows], unit_send.at[index], unit_recv.at[index], sibling)

    def project(index, buffer):
        rows = pl.ds(pl.multiple_of(index * UNIT, UNIT), UNIT)
        buffer[pl.ds(0, UNIT), :] = jnp.dot(feats[rows, :], proj[...], preferred_element_type=F32)
        feats_t[:, rows] = feats[rows, :].T

    def normalize(index, buffer):
        for i in range(UNIT // STEP):
            there = pl.ds(pl.multiple_of(index * UNIT + i * STEP, STEP), STEP)
            raw = buffer[pl.ds(i * STEP, STEP), :]
            inv = 1.0 / jnp.sqrt(jnp.sum(raw * raw, axis=1, keepdims=True) + 1e-06)
            value = raw * inv
            half = value.astype(BF16)
            unit[there, :] = half
            unit_low[there, :] = (value - half.astype(F32)).astype(BF16)
            inv_norm[there, :] = inv

    def three_units(first):
        project(first, wide)
        project(first + 1, perm)
        normalize(first, wide)
        unit_copy(first).start()
        project(first + 2, wide)
        normalize(first + 1, perm)
        unit_copy(first + 1).start()
        normalize(first + 2, wide)
        unit_copy(first + 2).start()

    scale = jnp.exp(jnp.full((1, TILE), log_scale[0], F32))
    slope = scale * LOG2E
    offset = jnp.full((1, TILE), logit_bias[0], F32) * LOG2E

    def tile_copy(t, a, b):
        return remote(
            pairs_t.at[t],
            pairs.at[pl.ds(pl.multiple_of(b * TILE, TILE), TILE), pl.ds(pl.multiple_of(a * TILE, TILE), TILE)],
            tile_send.at[t], tile_recv.at[t], sibling,
        )

    def tile_place(t):
        place = []
        for k in range(2):
            found = [jnp.int32(TILES[c][7][k]) for c in range(2)]
            for i in range(7):
                found = [jnp.where(t == i, TILES[c][i][k], found[c]) for c in range(2)]
            place.append(jnp.where(is_image, found[0], found[1]))
        return place

    def cosines(t, buffer):
        a, b = tile_place(t)
        rows = pl.ds(pl.multiple_of(a * TILE, TILE), TILE)
        cols = pl.ds(pl.multiple_of(b * TILE, TILE), TILE)
        buffer[pl.ds(0, TILE), pl.ds(0, TILE)] = lax.dot_general(
            unit[rows, :], other[cols, :], (((1,), (1,)), ((), ())), preferred_element_type=F32
        )

    def pair_terms(t, buffer, diagonal):
        a, b = tile_place(t)
        cols = pl.ds(pl.multiple_of(b * TILE, TILE), TILE)
        acc = [jnp.zeros((8, TILE), F32) for _ in range(3)]
        for i in range(TILE // STEP):
            cosine = buffer[pl.ds(i * STEP, STEP), pl.ds(0, TILE)]
            arg = cosine * slope + offset
            masked = diagonal and i < UNIT // STEP
            if masked:
                row = i * STEP + lax.broadcasted_iota(jnp.int32, (STEP, TILE), 0)
                col = lax.broadcasted_iota(jnp.int32, (STEP, TILE), 1) + core * ROWS
                sign = jnp.where(row == col, -1.0, 1.0).astype(F32)
                arg = arg * sign
            up = jnp.exp2(arg)
            whole = 1.0 + up
            inv = pl.reciprocal(whole, approx=True)
            inv = inv * (2.0 - whole * inv)
            grad = up * inv
            loss = jnp.log(whole) + (up - (whole - 1.0)) * inv
            if masked:
                grad = grad * sign
            pairs[pl.ds(pl.multiple_of(a * TILE + i * STEP, STEP), STEP), cols] = grad.astype(BF16)
            acc = [acc[0] + fold(loss), acc[1] + fold(grad * cosine), acc[2] + fold(grad)]
        for k in range(3):
            sums[k] += acc[k]

    def hand_over(t):
        a, b = tile_place(t)
        rows = pl.ds(pl.multiple_of(a * TILE, TILE), TILE)
        cols = pl.ds(pl.multiple_of(b * TILE, TILE), TILE)
        pairs_t[t] = pairs[rows, cols].T
        tile_copy(t, a, b).start()

    def two_tiles(i, carry):
        t = 2 * i
        cosines(t + 1, perm)
        pair_terms(t, wide, False)
        hand_over(t)

        @pl.when(i == 1)
        def _():
            for index in range(6, 8):
                unit_copy(index).wait_recv()

        cosines(t + 2, wide)
        pair_terms(t + 1, perm, False)
        hand_over(t + 1)
        return carry

    sums[...] = jnp.zeros_like(sums)
    project(0, wide)
    normalize(0, wide)
    unit_copy(0).start()
    arrived(0, 1, 0)
    sends[(1, 2)].start()
    sends[(2, 2)].start()
    arrived(0, 3, 0)
    sends[(2, 3)].start()
    arrived(1, 0, 0)
    arrived(1, 0, 1)
    sends[(0, 2)].start()
    sends[(1, 3)].start()
    arrived(0, 3, 1)
    sends[(0, 3)].start()
    arrived(0, 1, 1)
    three_units(1)
    arrived(1, 3, 1)
    sends[(0, 4)].start()
    arrived(1, 1, 0)
    sends[(1, 4)].start()
    for index in range(4):
        unit_copy(index).wait_recv()
    cosines(0, wide)
    cosines(1, perm)
    pair_terms(0, wide, True)
    hand_over(0)
    pair_terms(1, perm, False)
    hand_over(1)
    for key in ((0, 2, 0), (0, 2, 1), (1, 1, 1), (1, 3, 0)):
        arrived(*key)
    three_units(4)
    arrived(1, 2, 0)
    arrived(1, 2, 1)
    project(7, wide)
    normalize(7, wide)
    unit_copy(7).start()
    for index in range(4, 6):
        unit_copy(index).wait_recv()
    cosines(2, wide)
    lax.fori_loop(1, 3, two_tiles, 0)
    cosines(7, perm)
    pair_terms(6, wide, False)
    hand_over(6)
    pair_terms(7, perm, False)
    hand_over(7)

    def scalar_copies(stage):
        if stage == 3:
            return [remote(scalars.at[3, core], scalars.at[3, core], scalar_send.at[9], scalar_recv.at[9], sibling)]
        return [
            remote(
                scalars.at[stage, pos[stage]], scalars.at[stage, pos[stage]],
                scalar_send.at[stage * 3 + step - 1], scalar_recv.at[stage * 3 + step - 1], along(stage, step),
            )
            for step in (1, 2, 3)
        ]

    def scalar_start(stage, value):
        scalars[stage, pos[stage] if stage < 3 else core] = value
        for copy in scalar_copies(stage):
            copy.start()

    def scalar_finish(stage):
        for copy in scalar_copies(stage):
            copy.wait()
        if stage == 3:
            return scalars[3, 0] + scalars[3, 1]
        return (scalars[stage, 0] + scalars[stage, 1]) + (scalars[stage, 2] + scalars[stage, 3])

    lanes = [sums[k][:, 0:128] + sums[k][:, 128:256] + (sums[k][:, 256:384] + sums[k][:, 384:512]) for k in range(3)]
    scalar_start(0, jnp.concatenate(lanes, axis=0))

    for copy in sends.values():
        copy.wait_send()
    cross(text_feats).wait_send()
    for t in range(6):
        tile_copy(t, 0, 0).wait_recv()

    scale_row = jnp.exp(jnp.full((1, 1), log_scale[0], F32))

    def gradients(a, buffer):
        rows = pl.ds(pl.multiple_of(a * TILE, TILE), TILE)
        buffer[pl.ds(0, TILE), :] = jnp.dot(pairs[rows, :], other[...], preferred_element_type=F32)

    def tangents(a, buffer):
        for i in range(TILE // STEP):
            there = pl.ds(pl.multiple_of(a * TILE + i * STEP, STEP), STEP)
            grad = buffer[pl.ds(i * STEP, STEP), :]
            value = unit[there, :].astype(F32) + unit_low[there, :].astype(F32)
            inner = jnp.sum(value * grad, axis=1, keepdims=True)
            feats[there, :] = ((grad - value * inner) * (inv_norm[there, :] * scale_row)).astype(BF16)

    order = (1 - core, 3 - core, core, 2 + core)
    gradients(order[0], wide)
    gradients(order[1], perm)
    tangents(order[0], wide)
    for t in range(6, 8):
        tile_copy(t, 0, 0).wait_recv()
    gradients(order[2], wide)
    tangents(order[1], perm)
    gradients(order[3], perm)
    tangents(order[2], wide)
    tangents(order[3], perm)
    scalar_start(1, scalar_finish(0))

    def weights(t):
        cols = pl.ds(pl.multiple_of(t * THIRD, PART), THIRD)
        wide[:, cols] = jnp.dot(feats_t[...], feats[:, cols], preferred_element_type=F32)

    up = 1 - 2 * core

    def columns(t, p):
        return pl.ds(pl.multiple_of(t * THIRD + p * PART, PART), PART)

    def first_copies(t, p):
        axis, q = ORDERS[p][0], t * 3 + p
        ahead, behind = along(axis, lax.rem(4 + up, 4)), along(axis, lax.rem(4 - up, 4))
        return (
            remote(first_a.at[q], into_a.at[q], first_send.at[q, 0], first_recv.at[q, 0], ahead),
            remote(first_b.at[q], into_b.at[q], first_send.at[q, 1], first_recv.at[q, 1], behind),
            remote(into_a.at[q], into_c.at[q], first_send.at[q, 2], first_recv.at[q, 2], ahead),
        )

    def block(t, p, step):
        k = lax.rem(pos[ORDERS[p][0]] + 4 + step, 4)
        return pl.ds(pl.multiple_of(k * 288, 288), 288), columns(t, p)

    def first_start(t, p):
        for k1 in range(4):
            for k2 in range(4):
                for k3 in range(4):
                    place = [0, 0, 0]
                    for axis, k in zip(ORDERS[p], (k1, k2, k3)):
                        place[axis] = k
                    perm[pl.ds(k1 * 288 + k2 * 72 + k3 * 18, 18), columns(t, p)] = (
                        wide[pl.ds(natural_row(*place), 18), columns(t, p)])
        q = t * 3 + p
        first_a[q] = perm[block(t, p, 2)].astype(BF16)
        first_b[q] = perm[block(t, p, -up)].astype(BF16)
        copies = first_copies(t, p)
        copies[0].start()
        copies[1].start()

    def first_forward(t, p):
        copies, q = first_copies(t, p), t * 3 + p
        copies[0].wait_recv()
        into_a[q] = (perm[block(t, p, up)] + into_a[q].astype(F32)).astype(BF16)
        copies[2].start()

    def second_copies(t, p):
        q = t * 3 + p
        return [
            remote(second_out.at[q, step - 1], second_in.at[q, step - 1], second_send.at[q, step - 1],
                   second_recv.at[q, step - 1], along(ORDERS[p][1], step))
            for step in (1, 2, 3)
        ]

    def second_rows(p, step):
        return pl.ds(pl.multiple_of(lax.rem(pos[ORDERS[p][1]] + step, 4) * 72, 8), 72)

    def second_start(t, p):
        copies, q = first_copies(t, p), t * 3 + p
        copies[1].wait_recv()
        copies[2].wait_recv()
        part_sum[q] = perm[block(t, p, 0)] + into_b[q].astype(F32) + into_c[q].astype(F32)
        for step, copy in zip((1, 2, 3), second_copies(t, p)):
            second_out[q, step - 1, pl.ds(0, 72), :] = part_sum[q, second_rows(p, step), :].astype(BF16)
            copy.start()

    def third_copies(t, p):
        axis, q = ORDERS[p][2], t * 3 + p
        copies = []
        for flip in (False, True):
            half = 1 - core if flip else core
            for step in range(4):
                if step or flip:
                    sem = 3 + step if flip else step - 1
                    copies.append(remote(
                        third_own.at[q, lax.rem(pos[axis] + step, 4), half], third_in.at[q, core, step],
                        third_send.at[q, sem], third_recv.at[q, sem], along(axis, step, flip)))
        return copies

    def third_start(t, p):
        q = t * 3 + p
        total = part_sum[q, second_rows(p, 0), :]
        for step, copy in zip((1, 2, 3), second_copies(t, p)):
            copy.wait_recv()
            total += second_in[q, step - 1, pl.ds(0, 72), :].astype(F32)
        part_sum[q, pl.ds(0, 72), :] = total
        for k in range(4):
            for h in range(2):
                third_own[q, k, h, pl.ds(0, 9), :] = part_sum[q, pl.ds(18 * k + 9 * h, 9), :]
        for copy in third_copies(t, p):
            copy.start()
        third_in[q, core, 0] = third_own[q, pos[ORDERS[p][2]], core]

    def third_finish(t, p):
        q = t * 3 + p
        for copy in third_copies(t, p):
            copy.wait_recv()
        for side in range(2):
            got = [third_in[q, side, step, pl.ds(0, 9), :] for step in range(4)]
            out[pl.ds(16 * side, 9), columns(t, p)] = (got[0] + got[1]) + (got[2] + got[3])

    def each(step, t):
        for p in range(3):
            step(t, p)

    def third(t, carry):
        weights(t)

        @pl.when(t > 0)
        def _():
            each(first_forward, t - 1)

        each(first_start, t)

        @pl.when(t > 1)
        def _():
            each(second_start, t - 2)

        return carry

    lax.fori_loop(0, 3, third, 0)
    scalar_start(2, scalar_finish(1))
    each(first_forward, 2)
    each(second_start, 1)
    each(third_start, 0)
    each(second_start, 2)
    scalar_start(3, scalar_finish(2))
    each(third_start, 1)
    each(third_finish, 0)
    each(third_start, 2)
    each(third_finish, 1)
    totals = scalar_finish(3)
    batch = 1.0 / 16384.0
    row_scale = jnp.exp(jnp.full((8, 128), log_scale[0], F32))
    for k, value in enumerate((totals[0:8], totals[8:16] * row_scale, totals[16:24])):
        out[pl.ds(9 + k, 1), pl.ds(0, 128)] = jnp.full((1, 128), jnp.sum(value) * batch, F32)
    each(third_finish, 2)

    def sent(t, carry):
        for p in range(3):
            for copy in first_copies(t, p) + tuple(second_copies(t, p)) + tuple(third_copies(t, p)):
                copy.wait_send()
        return carry

    lax.fori_loop(0, 3, sent, 0)
    for index in range(8):
        unit_copy(index).wait_send()
        tile_copy(index, 0, 0).wait_send()

def split(packed, loss_out, image_out, text_out, scale_out, bias_out):
    image_out[...] = packed[pl.ds(0, 9), :]
    text_out[...] = packed[pl.ds(16, 9), :]
    loss_out[0] = packed[9, 0]
    scale_out[0] = packed[10, 0]
    bias_out[0] = packed[11, 0]


def per_device(image_feats, text_feats, image_proj, text_proj, log_scale, logit_bias):
    smem = pl.BlockSpec(memory_space=pltpu.SMEM)
    vmem = pl.BlockSpec(memory_space=pltpu.VMEM)
    hbm = pl.BlockSpec(memory_space=pl.ANY)
    dma, buffer = pltpu.SemaphoreType.DMA, pltpu.VMEM
    one = jax.ShapeDtypeStruct((1,), F32)
    rows = jax.ShapeDtypeStruct((9, WIDTH), F32)
    packed = pl.pallas_call(
        kernel,
        out_shape=jax.ShapeDtypeStruct((32, WIDTH), F32),
        in_specs=[smem, smem, hbm, hbm, hbm, hbm],
        out_specs=vmem,
        scratch_shapes=[
            buffer((ROWS, WIDTH), BF16),
            buffer((WIDTH, ROWS), BF16),
            buffer((ROWS, WIDTH), BF16),
            buffer((ROWS, WIDTH), BF16),
            buffer((ROWS, WIDTH), BF16),
            buffer((ROWS, ROWS), BF16),
            buffer((8, TILE, TILE), BF16),
            buffer((WIDTH, WIDTH), BF16),
            buffer((ROWS, 1), F32),
            buffer((WIDTH, WIDTH), F32),
            buffer((WIDTH, WIDTH), F32),
            buffer((3, 8, TILE), F32),
            *[buffer((9, 288, PART), BF16) for _ in range(5)],
            buffer((9, 288, PART), F32),
            buffer((9, 3, 80, PART), BF16),
            buffer((9, 3, 80, PART), BF16),
            buffer((9, 4, 2, 16, PART), F32),
            buffer((9, 2, 4, 16, PART), F32),
            buffer((4, 4, 24, 128), F32),
            dma((2,)),
            dma((15,)), dma((16,)),
            dma((8,)), dma((8,)),
            dma((8,)), dma((8,)),
            *[dma((9, 3)) for _ in range(4)],
            dma((9, 7)), dma((9, 7)),
            dma((10,)), dma((10,)),
        ],
        compiler_params=pltpu.CompilerParams(collective_id=0, has_side_effects=True, vmem_limit_bytes=63 * 2**20),
        name="sigmoid_loss",
    )(log_scale, logit_bias, image_feats, text_feats, image_proj, text_proj)
    return pl.pallas_call(
        split,
        out_shape=(one, rows, rows, one, one),
        in_specs=[vmem],
        out_specs=(smem, vmem, vmem, smem, smem),
        name="split_outputs",
    )(packed)


def solution(mesh):
    return jax.shard_map(
        per_device,
        mesh=mesh,
        in_specs=(P(("dp", "mp"), None), P(("dp", "mp"), None), P(), P(), P(), P()),
        out_specs=(P(), P(("dp", "mp"), None), P(("dp", "mp"), None), P(), P()),
        check_vma=False,
    )
```

```python
import functools

import jax
import jax.numpy as jnp
from jax import lax
from jax.experimental import pallas as pl
from jax.experimental.pallas import tpu as pltpu
from jax.sharding import PartitionSpec as P

MESH = pl.DeviceIdType.MESH
BF16, F32 = jnp.bfloat16, jnp.float32
WIDTH = 1152
OWN = 128
UNIT = 2 * OWN
ROWS = 8 * UNIT
TILE = 512
PART = 128
STEP = 16
LOG2E = 1.4426950408889634

UNITS = {(0, 0): 0, (1, 0): 1, (0, 3): 2, (0, 1): 3, (1, 3): 4, (1, 1): 5, (0, 2): 6, (1, 2): 7}
RING_UP = [((0, 0, 0), (0, 3, 0)), ((0, 0, 1), (0, 3, 1)), ((0, 3, 0), (0, 2, 0)), ((1, 0, 1), (1, 3, 1)), ((1, 3, 0), (1, 2, 0))]
RING_DOWN = [((0, 0, 0), (0, 1, 0)), ((0, 0, 1), (0, 1, 1)), ((1, 0, 1), (1, 1, 1)), ((0, 1, 1), (0, 2, 1)), ((1, 1, 1), (1, 2, 1))]
ACROSS = [((0, 0, 1), (1, 0, 1)), ((0, 0, 0), (1, 0, 0)), ((0, 3, 0), (1, 3, 0)), ((0, 1, 0), (1, 1, 0))]
TILES = [
    [(0, 0), (1, 1), (0, 2), (2, 0), (2, 2), (1, 3), (3, 1), (3, 3)],
    [(0, 1), (1, 0), (1, 2), (2, 1), (0, 3), (2, 3), (3, 0), (3, 2)],
]
ORDERS = [(0, 1, 2), (1, 2, 0), (2, 0, 1)]

BATCHES = [(0, 3, 6), (1, 4), (2, 5), (7,), (8,)]
SECOND = [(0, 240), (240, 160), (400, 160), (560, 80), (640, 80)]
THIRD = [(0, 32), (32, 24), (56, 24), (80, 16), (96, 16)]


def device(x, y, z, core):
    x, y, z = lax.rem(x, 4), lax.rem(y, 4), lax.rem(z, 4)
    return (lax.rem(z, 2) * 16 + x * 4 + y, lax.div(z, 2) * 2 + core)


def natural_row(x, y, z):
    return 18 * (((z % 2) * 16 + x * 4 + y) * 2 + z // 2)


def fold(v):
    return v[0:8] + v[8:16]


def kernel(
    log_scale, logit_bias, image_feats, text_feats, image_proj, text_proj,
    out,
    feats, feats_t, unit, unit_low, other, pairs, pairs_t, proj, inv_norm, wide, perm, sums,
    first_a, first_b, into_a, into_b, into_c, part_sum, second_out, second_in, third_own, third_in,
    scalars,
    local_sem, gather_send, gather_recv, unit_send, unit_recv, tile_send, tile_recv,
    first_send, first_recv, second_send, second_recv, third_send, third_recv, scalar_send, scalar_recv,
):
    dp, mp = lax.axis_index("dp"), lax.axis_index("mp")
    core = lax.rem(mp, 2)
    x = lax.rem(lax.div(dp, 4), 4)
    y = lax.rem(dp, 4)
    z = lax.div(mp, 2) * 2 + lax.div(dp, 16)
    pos = (x, y, z)
    is_image = core == 0
    sibling = (dp, mp + 1 - 2 * core)

    def along(axis, step, other_core=False):
        moved = [x, y, z]
        moved[axis] = moved[axis] + step
        return device(*moved, 1 - core if other_core else core)

    def ring(step):
        return device(jnp.where(is_image, x, x + step), y, jnp.where(is_image, z + step, z), core)

    even = lax.rem(y, 2) == 0
    across = device(x, jnp.where(is_image == even, y + 1, y + 3), z, core)

    def remote(src, dst, send, recv, to):
        return pltpu.make_async_remote_copy(
            src_ref=src, dst_ref=dst, send_sem=send, recv_sem=recv, device_id=to, device_id_type=MESH
        )

    def slot(key):
        dy, dr, half = key
        side = core if half == 0 else 1 - core
        return pl.ds(pl.multiple_of(UNITS[(dy, dr)] * UNIT + side * OWN, OWN), OWN)

    def arrival(key):
        return gather_recv.at[UNITS[key[:2]] * 2 + key[2]]

    own = slot((0, 0, 0))
    own_copy = pltpu.make_async_copy(image_feats, feats.at[own], local_sem.at[0])
    proj_copy = pltpu.make_async_copy(image_proj, proj, local_sem.at[1])

    @pl.when(is_image)
    def _():
        own_copy.start()
        proj_copy.start()

    @pl.when(jnp.logical_not(is_image))
    def _():
        pltpu.make_async_copy(text_feats, feats.at[own], local_sem.at[0]).start()
        pltpu.make_async_copy(text_proj, proj, local_sem.at[1]).start()

    barrier = pltpu.get_barrier_semaphore()
    known = {(axis, step, flip): along(axis, step, flip) for axis in range(3) for step in (1, 2, 3) for flip in (False, True)}
    partners = list(known.values()) + [sibling]
    for partner in partners:
        pl.semaphore_signal(barrier, inc=1, device_id=partner, device_id_type=MESH)
    pl.semaphore_wait(barrier, len(partners))

    def cross(src):
        return remote(src, feats.at[own], gather_send.at[14], gather_recv.at[1], sibling)

    @pl.when(is_image)
    def _():
        cross(text_feats).start()

    @pl.when(jnp.logical_not(is_image))
    def _():
        cross(image_feats).start()

    own_copy.wait()

    sends = {}
    for index, (path, to) in enumerate(((RING_UP, ring(1)), (RING_DOWN, ring(3)), (ACROSS, across))):
        for step, (source, target) in enumerate(path):
            sends[(index, step)] = remote(
                feats.at[slot(source)], feats.at[slot(target)], gather_send.at[index * 5 + step], arrival(target), to
            )

    def arrived(*key):
        remote(feats.at[slot(key)], feats.at[slot(key)], gather_send.at[0], arrival(key), sibling).wait_recv()

    sends[(0, 0)].start()
    sends[(1, 0)].start()
    arrived(0, 0, 1)
    sends[(2, 0)].start()
    sends[(0, 1)].start()
    sends[(1, 1)].start()
    sends[(2, 1)].start()
    proj_copy.wait()

    def unit_copy(index):
        rows = pl.ds(pl.multiple_of(index * UNIT, UNIT), UNIT)
        return remote(unit.at[rows], other.at[rows], unit_send.at[index], unit_recv.at[index], sibling)

    def project(index, buffer):
        rows = pl.ds(pl.multiple_of(index * UNIT, UNIT), UNIT)
        buffer[pl.ds(0, UNIT), :] = jnp.dot(feats[rows, :], proj[...], preferred_element_type=F32)
        feats_t[:, rows] = feats[rows, :].T

    def normalize(index, buffer):
        for i in range(UNIT // STEP):
            there = pl.ds(pl.multiple_of(index * UNIT + i * STEP, STEP), STEP)
            raw = buffer[pl.ds(i * STEP, STEP), :]
            inv = 1.0 / jnp.sqrt(jnp.sum(raw * raw, axis=1, keepdims=True) + 1e-06)
            value = raw * inv
            half = value.astype(BF16)
            unit[there, :] = half
            unit_low[there, :] = (value - half.astype(F32)).astype(BF16)
            inv_norm[there, :] = inv

    def three_units(units, ready):
        project(units[0], wide)
        project(units[1], perm)
        normalize(units[0], wide)
        unit_copy(units[0]).start()
        normalize(units[1], perm)
        unit_copy(units[1]).start()
        for key in ready:
            arrived(*key)
        project(units[2], wide)
        normalize(units[2], wide)
        unit_copy(units[2]).start()

    scale = jnp.exp(jnp.full((1, TILE), log_scale[0], F32))
    slope = scale * LOG2E
    offset = jnp.full((1, TILE), logit_bias[0], F32) * LOG2E

    def tile_copy(t, a, b):
        return remote(
            pairs_t.at[t],
            pairs.at[pl.ds(pl.multiple_of(b * TILE, TILE), TILE), pl.ds(pl.multiple_of(a * TILE, TILE), TILE)],
            tile_send.at[t], tile_recv.at[t], sibling,
        )

    def tile_place(t):
        place = []
        for k in range(2):
            found = [jnp.int32(TILES[c][7][k]) for c in range(2)]
            for i in range(7):
                found = [jnp.where(t == i, TILES[c][i][k], found[c]) for c in range(2)]
            place.append(jnp.where(is_image, found[0], found[1]))
        return place

    def cosines(t, buffer):
        a, b = tile_place(t)
        rows = pl.ds(pl.multiple_of(a * TILE, TILE), TILE)
        cols = pl.ds(pl.multiple_of(b * TILE, TILE), TILE)
        buffer[pl.ds(0, TILE), pl.ds(0, TILE)] = lax.dot_general(
            unit[rows, :], other[cols, :], (((1,), (1,)), ((), ())), preferred_element_type=F32
        )

    def pair_terms(t, buffer, diagonal):
        a, b = tile_place(t)
        cols = pl.ds(pl.multiple_of(b * TILE, TILE), TILE)
        acc = [jnp.zeros((8, TILE), F32) for _ in range(3)]
        for i in range(TILE // STEP):
            cosine = buffer[pl.ds(i * STEP, STEP), pl.ds(0, TILE)]
            arg = cosine * slope + offset
            masked = diagonal and i < UNIT // STEP
            if masked:
                row = i * STEP + lax.broadcasted_iota(jnp.int32, (STEP, TILE), 0)
                col = lax.broadcasted_iota(jnp.int32, (STEP, TILE), 1) + core * ROWS
                sign = jnp.where(row == col, -1.0, 1.0).astype(F32)
                arg = arg * sign
            up = jnp.exp2(arg)
            whole = 1.0 + up
            inv = pl.reciprocal(whole, approx=True)
            inv = inv * (2.0 - whole * inv)
            grad = up * inv
            loss = jnp.log(whole) + (up - (whole - 1.0)) * inv
            if masked:
                grad = grad * sign
            pairs[pl.ds(pl.multiple_of(a * TILE + i * STEP, STEP), STEP), cols] = grad.astype(BF16)
            acc = [acc[0] + fold(loss), acc[1] + fold(grad * cosine), acc[2] + fold(grad)]
        for k in range(3):
            sums[k] += acc[k]

    def hand_over(t):
        a, b = tile_place(t)
        rows = pl.ds(pl.multiple_of(a * TILE, TILE), TILE)
        cols = pl.ds(pl.multiple_of(b * TILE, TILE), TILE)
        pairs_t[t] = pairs[rows, cols].T
        tile_copy(t, a, b).start()

    def two_tiles(i, carry):
        t = 2 * i
        cosines(t + 1, perm)
        pair_terms(t, wide, False)
        hand_over(t)

        @pl.when(i == 1)
        def _():
            for index in range(6, 8):
                unit_copy(index).wait_recv()

        cosines(t + 2, wide)
        pair_terms(t + 1, perm, False)
        hand_over(t + 1)
        return carry

    sums[...] = jnp.zeros_like(sums)
    project(0, wide)
    normalize(0, wide)
    unit_copy(0).start()
    arrived(0, 3, 0)
    sends[(0, 2)].start()
    sends[(2, 2)].start()
    arrived(0, 1, 0)
    sends[(2, 3)].start()
    arrived(1, 0, 1)
    sends[(1, 2)].start()
    sends[(0, 3)].start()
    arrived(0, 1, 1)
    sends[(1, 3)].start()
    arrived(0, 3, 1)
    three_units((2, 3, 1), [(1, 0, 0)])
    arrived(1, 1, 1)
    sends[(1, 4)].start()
    arrived(1, 3, 0)
    sends[(0, 4)].start()
    for index in range(4):
        unit_copy(index).wait_recv()
    cosines(0, wide)
    cosines(1, perm)
    pair_terms(0, wide, True)
    hand_over(0)
    pair_terms(1, perm, False)
    hand_over(1)
    for key in ((1, 3, 1), (0, 2, 0), (0, 2, 1)):
        arrived(*key)
    three_units((4, 6, 5), [(1, 1, 0)])
    arrived(1, 2, 0)
    arrived(1, 2, 1)
    project(7, wide)
    normalize(7, wide)
    unit_copy(7).start()
    for index in range(4, 6):
        unit_copy(index).wait_recv()
    cosines(2, wide)
    lax.fori_loop(1, 3, two_tiles, 0)
    cosines(7, perm)
    pair_terms(6, wide, False)
    hand_over(6)
    pair_terms(7, perm, False)
    hand_over(7)

    def scalar_copies(stage):
        if stage == 3:
            return [remote(scalars.at[3, core], scalars.at[3, core], scalar_send.at[9], scalar_recv.at[9], sibling)]
        return [
            remote(
                scalars.at[stage, pos[stage]], scalars.at[stage, pos[stage]],
                scalar_send.at[stage * 3 + step - 1], scalar_recv.at[stage * 3 + step - 1], along(stage, step),
            )
            for step in (1, 2, 3)
        ]

    def scalar_start(stage, value):
        scalars[stage, pos[stage] if stage < 3 else core] = value
        for copy in scalar_copies(stage):
            copy.start()

    def scalar_finish(stage):
        for copy in scalar_copies(stage):
            copy.wait()
        if stage == 3:
            return scalars[3, 0] + scalars[3, 1]
        return (scalars[stage, 0] + scalars[stage, 1]) + (scalars[stage, 2] + scalars[stage, 3])

    lanes = [sums[k][:, 0:128] + sums[k][:, 128:256] + (sums[k][:, 256:384] + sums[k][:, 384:512]) for k in range(3)]
    scalar_start(0, jnp.concatenate(lanes, axis=0))

    for copy in sends.values():
        copy.wait_send()
    cross(text_feats).wait_send()
    for t in range(6):
        tile_copy(t, 0, 0).wait_recv()

    scale_row = jnp.exp(jnp.full((1, 1), log_scale[0], F32))

    def gradients(a, buffer):
        rows = pl.ds(pl.multiple_of(a * TILE, TILE), TILE)
        buffer[pl.ds(0, TILE), :] = jnp.dot(pairs[rows, :], other[...], preferred_element_type=F32)

    def tangents(a, buffer):
        for i in range(TILE // STEP):
            there = pl.ds(pl.multiple_of(a * TILE + i * STEP, STEP), STEP)
            grad = buffer[pl.ds(i * STEP, STEP), :]
            value = unit[there, :].astype(F32) + unit_low[there, :].astype(F32)
            inner = jnp.sum(value * grad, axis=1, keepdims=True)
            feats[there, :] = ((grad - value * inner) * (inv_norm[there, :] * scale_row)).astype(BF16)

    order = (1 - core, 3 - core, core, 2 + core)
    gradients(order[0], wide)
    gradients(order[1], perm)
    tangents(order[0], wide)
    for t in range(6, 8):
        tile_copy(t, 0, 0).wait_recv()
    gradients(order[2], wide)
    tangents(order[1], perm)
    gradients(order[3], perm)
    tangents(order[2], wide)
    tangents(order[3], perm)
    scalar_start(1, scalar_finish(0))

    def weights(parts):
        cols = pl.ds(parts[0] * PART, len(parts) * PART)
        wide[:, cols] = jnp.dot(feats_t[...], feats[:, cols], preferred_element_type=F32)

    up = 1 - 2 * core

    def columns(q):
        return pl.ds(q * PART, PART)

    def first_copies(q):
        axis = ORDERS[q % 3][0]
        ahead, behind = along(axis, lax.rem(4 + up, 4)), along(axis, lax.rem(4 - up, 4))
        return (
            remote(first_a.at[q], into_a.at[q], first_send.at[q, 0], first_recv.at[q, 0], ahead),
            remote(first_b.at[q], into_b.at[q], first_send.at[q, 1], first_recv.at[q, 1], behind),
            remote(into_a.at[q], into_c.at[q], first_send.at[q, 2], first_recv.at[q, 2], ahead),
        )

    def block(q, step):
        k = lax.rem(pos[ORDERS[q % 3][0]] + 4 + step, 4)
        return pl.ds(pl.multiple_of(k * 288, 288), 288), columns(q)

    def first_start(q):
        for k1 in range(4):
            for k2 in range(4):
                for k3 in range(4):
                    place = [0, 0, 0]
                    for axis, k in zip(ORDERS[q % 3], (k1, k2, k3)):
                        place[axis] = k
                    perm[pl.ds(k1 * 288 + k2 * 72 + k3 * 18, 18), columns(q)] = (
                        wide[pl.ds(natural_row(*place), 18), columns(q)])
        first_a[q] = perm[block(q, 2)].astype(BF16)
        first_b[q] = perm[block(q, -up)].astype(BF16)
        copies = first_copies(q)
        copies[0].start()
        copies[1].start()

    def first_forward(q):
        copies = first_copies(q)
        copies[0].wait_recv()
        into_a[q] = (perm[block(q, up)] + into_a[q].astype(F32)).astype(BF16)
        copies[2].start()

    def second_copies(b):
        start, size = SECOND[b]
        return [
            remote(second_out.at[step - 1, pl.ds(start, size)], second_in.at[step - 1, pl.ds(start, size)],
                   second_send.at[b, step - 1], second_recv.at[b, step - 1], known[ORDERS[BATCHES[b][0] % 3][1], step, False])
            for step in (1, 2, 3)
        ]

    def second_rows(q, step):
        return pl.ds(pl.multiple_of(lax.rem(pos[ORDERS[q % 3][1]] + step, 4) * 72, 8), 72)

    def second_start(b):
        for i, q in enumerate(BATCHES[b]):
            copies = first_copies(q)
            copies[1].wait_recv()
            copies[2].wait_recv()
            part_sum[q] = perm[block(q, 0)] + into_b[q].astype(F32) + into_c[q].astype(F32)
            for step in (1, 2, 3):
                second_out[step - 1, pl.ds(SECOND[b][0] + 80 * i, 72), :] = part_sum[q, second_rows(q, step), :].astype(BF16)
        for copy in second_copies(b):
            copy.start()

    def third_copies(b):
        axis = ORDERS[BATCHES[b][0] % 3][2]
        rows = pl.ds(*THIRD[b])
        copies = []
        for flip in (False, True):
            half = 1 - core if flip else core
            for step in range(4):
                if step or flip:
                    sem = 3 + step if flip else step - 1
                    copies.append(remote(
                        third_own.at[lax.rem(pos[axis] + step, 4), half, rows], third_in.at[core, step, rows],
                        third_send.at[b, sem], third_recv.at[b, sem], known[axis, step, flip] if step else sibling))
        return copies

    def third_start(b):
        for copy in second_copies(b):
            copy.wait_recv()
        for i, q in enumerate(BATCHES[b]):
            total = part_sum[q, second_rows(q, 0), :]
            for step in (1, 2, 3):
                total += second_in[step - 1, pl.ds(SECOND[b][0] + 80 * i, 72), :].astype(F32)
            part_sum[q, pl.ds(0, 72), :] = total
            for k in range(4):
                for h in range(2):
                    third_own[k, h, pl.ds(THIRD[b][0] + 9 * i, 9), :] = part_sum[q, pl.ds(18 * k + 9 * h, 9), :]
        for copy in third_copies(b):
            copy.start()
        rows = pl.ds(*THIRD[b])
        third_in[core, 0, rows] = third_own[pos[ORDERS[BATCHES[b][0] % 3][2]], core, rows]

    def third_finish(b):
        for copy in third_copies(b):
            copy.wait_recv()
        for i, q in enumerate(BATCHES[b]):
            for side in range(2):
                got = [third_in[side, step, pl.ds(THIRD[b][0] + 9 * i, 9), :] for step in range(4)]
                out[pl.ds(16 * side, 9), columns(q)] = (got[0] + got[1]) + (got[2] + got[3])

    def each(step, parts):
        for q in parts:
            step(q)

    early, middle, late = range(0, 4), range(4, 7), range(7, 9)
    weights(early)
    each(first_start, early)
    weights(middle)
    each(first_start, middle)
    each(first_forward, early)
    weights(late)
    each(first_start, late)
    each(first_forward, middle)
    scalar_start(2, scalar_finish(1))
    each(first_forward, late)
    each(second_start, range(0, 3))
    each(second_start, range(3, 5))
    scalar_start(3, scalar_finish(2))
    each(third_start, range(0, 3))
    each(third_start, range(3, 5))
    totals = scalar_finish(3)
    batch = 1.0 / 16384.0
    row_scale = jnp.exp(jnp.full((8, 128), log_scale[0], F32))
    for k, value in enumerate((totals[0:8], totals[8:16] * row_scale, totals[16:24])):
        out[pl.ds(9 + k, 1), pl.ds(0, 128)] = jnp.full((1, 128), jnp.sum(value) * batch, F32)
    each(third_finish, range(5))

    for q in range(9):
        for copy in first_copies(q):
            copy.wait_send()
    for b in range(5):
        for copy in second_copies(b) + third_copies(b):
            copy.wait_send()
    for index in range(8):
        unit_copy(index).wait_send()
        tile_copy(index, 0, 0).wait_send()

def split(packed, loss_out, image_out, text_out, scale_out, bias_out):
    image_out[...] = packed[pl.ds(0, 9), :]
    text_out[...] = packed[pl.ds(16, 9), :]
    loss_out[0] = packed[9, 0]
    scale_out[0] = packed[10, 0]
    bias_out[0] = packed[11, 0]


def per_device(image_feats, text_feats, image_proj, text_proj, log_scale, logit_bias):
    smem = pl.BlockSpec(memory_space=pltpu.SMEM)
    vmem = pl.BlockSpec(memory_space=pltpu.VMEM)
    hbm = pl.BlockSpec(memory_space=pl.ANY)
    dma, buffer = pltpu.SemaphoreType.DMA, pltpu.VMEM
    one = jax.ShapeDtypeStruct((1,), F32)
    rows = jax.ShapeDtypeStruct((9, WIDTH), F32)
    packed = pl.pallas_call(
        kernel,
        out_shape=jax.ShapeDtypeStruct((32, WIDTH), F32),
        in_specs=[smem, smem, hbm, hbm, hbm, hbm],
        out_specs=vmem,
        scratch_shapes=[
            buffer((ROWS, WIDTH), BF16),
            buffer((WIDTH, ROWS), BF16),
            buffer((ROWS, WIDTH), BF16),
            buffer((ROWS, WIDTH), BF16),
            buffer((ROWS, WIDTH), BF16),
            buffer((ROWS, ROWS), BF16),
            buffer((8, TILE, TILE), BF16),
            buffer((WIDTH, WIDTH), BF16),
            buffer((ROWS, 1), F32),
            buffer((WIDTH, WIDTH), F32),
            buffer((WIDTH, WIDTH), F32),
            buffer((3, 8, TILE), F32),
            *[buffer((9, 288, PART), BF16) for _ in range(5)],
            buffer((9, 288, PART), F32),
            buffer((3, 720, PART), BF16),
            buffer((3, 720, PART), BF16),
            buffer((4, 2, 112, PART), F32),
            buffer((2, 4, 112, PART), F32),
            buffer((4, 4, 24, 128), F32),
            dma((2,)),
            dma((15,)), dma((16,)),
            dma((8,)), dma((8,)),
            dma((8,)), dma((8,)),
            dma((9, 3)), dma((9, 3)), dma((5, 3)), dma((5, 3)), dma((5, 7)), dma((5, 7)),
            dma((10,)), dma((10,)),
        ],
        compiler_params=pltpu.CompilerParams(collective_id=0, has_side_effects=True, vmem_limit_bytes=63 * 2**20),
        name="sigmoid_loss",
    )(log_scale, logit_bias, image_feats, text_feats, image_proj, text_proj)
    return pl.pallas_call(
        split,
        out_shape=(one, rows, rows, one, one),
        in_specs=[vmem],
        out_specs=(smem, vmem, vmem, smem, smem),
        name="split_outputs",
    )(packed)


def solution(mesh):
    return jax.shard_map(
        per_device,
        mesh=mesh,
        in_specs=(P(("dp", "mp"), None), P(("dp", "mp"), None), P(), P(), P(), P()),
        out_specs=(P(), P(("dp", "mp"), None), P(("dp", "mp"), None), P(), P()),
        check_vma=False,
    )
```

```python
import functools

import jax
import jax.numpy as jnp
from jax import lax
from jax.experimental import pallas as pl
from jax.experimental.pallas import tpu as pltpu
from jax.sharding import PartitionSpec as P

MESH = pl.DeviceIdType.MESH
BF16, F32 = jnp.bfloat16, jnp.float32
WIDTH = 1152
OWN = 128
UNIT = 2 * OWN
ROWS = 8 * UNIT
TILE = 512
PART = 128
STEP = 16
LOG2E = 1.4426950408889634

UNITS = {(0, 0): 0, (1, 0): 1, (0, 3): 2, (0, 1): 3, (1, 3): 4, (1, 1): 5, (0, 2): 6, (1, 2): 7}
RING_UP = [((0, 0, 0), (0, 3, 0)), ((0, 0, 1), (0, 3, 1)), ((0, 3, 0), (0, 2, 0)), ((1, 0, 1), (1, 3, 1)), ((1, 3, 0), (1, 2, 0))]
RING_DOWN = [((0, 0, 0), (0, 1, 0)), ((0, 0, 1), (0, 1, 1)), ((1, 0, 1), (1, 1, 1)), ((0, 1, 1), (0, 2, 1)), ((1, 1, 1), (1, 2, 1))]
ACROSS = [((0, 0, 1), (1, 0, 1)), ((0, 0, 0), (1, 0, 0)), ((0, 3, 0), (1, 3, 0)), ((0, 1, 0), (1, 1, 0))]
TILES = [
    [(0, 0), (1, 1), (0, 2), (2, 0), (2, 2), (1, 3), (3, 1), (3, 3)],
    [(0, 1), (1, 0), (1, 2), (2, 1), (0, 3), (2, 3), (3, 0), (3, 2)],
]
ORDERS = [(0, 1, 2), (1, 2, 0), (2, 0, 1)]

BATCHES = [(0, 3, 6), (1, 4, 7), (2, 5), (8,)]
SECOND = [(0, 240), (240, 240), (480, 160), (640, 80)]
THIRD = [(0, 32), (32, 32), (64, 24), (88, 16)]


def device(x, y, z, core):
    x, y, z = lax.rem(x, 4), lax.rem(y, 4), lax.rem(z, 4)
    return (lax.rem(z, 2) * 16 + x * 4 + y, lax.div(z, 2) * 2 + core)


def natural_row(x, y, z):
    return 18 * (((z % 2) * 16 + x * 4 + y) * 2 + z // 2)


def fold(v):
    return v[0:8] + v[8:16]


def kernel(
    log_scale, logit_bias, image_feats, text_feats, image_proj, text_proj,
    out,
    feats, feats_t, unit, unit_low, other, pairs, pairs_t, proj, inv_norm, wide, perm, sums,
    first_a, first_b, into_a, into_b, into_c, part_sum, second_out, second_in, third_own, third_in,
    scalars,
    local_sem, gather_send, gather_recv, unit_send, unit_recv, tile_send, tile_recv,
    first_send, first_recv, second_send, second_recv, third_send, third_recv, scalar_send, scalar_recv,
):
    dp, mp = lax.axis_index("dp"), lax.axis_index("mp")
    core = lax.rem(mp, 2)
    x = lax.rem(lax.div(dp, 4), 4)
    y = lax.rem(dp, 4)
    z = lax.div(mp, 2) * 2 + lax.div(dp, 16)
    pos = (x, y, z)
    is_image = core == 0
    sibling = (dp, mp + 1 - 2 * core)

    def along(axis, step, other_core=False):
        moved = [x, y, z]
        moved[axis] = moved[axis] + step
        return device(*moved, 1 - core if other_core else core)

    def ring(step):
        return device(jnp.where(is_image, x, x + step), y, jnp.where(is_image, z + step, z), core)

    even = lax.rem(y, 2) == 0
    across = device(x, jnp.where(is_image == even, y + 1, y + 3), z, core)

    def remote(src, dst, send, recv, to):
        return pltpu.make_async_remote_copy(
            src_ref=src, dst_ref=dst, send_sem=send, recv_sem=recv, device_id=to, device_id_type=MESH
        )

    def slot(key):
        dy, dr, half = key
        side = core if half == 0 else 1 - core
        return pl.ds(pl.multiple_of(UNITS[(dy, dr)] * UNIT + side * OWN, OWN), OWN)

    def arrival(key):
        return gather_recv.at[UNITS[key[:2]] * 2 + key[2]]

    own = slot((0, 0, 0))
    own_copy = pltpu.make_async_copy(image_feats, feats.at[own], local_sem.at[0])
    proj_copy = pltpu.make_async_copy(image_proj, proj, local_sem.at[1])

    @pl.when(is_image)
    def _():
        own_copy.start()
        proj_copy.start()

    @pl.when(jnp.logical_not(is_image))
    def _():
        pltpu.make_async_copy(text_feats, feats.at[own], local_sem.at[0]).start()
        pltpu.make_async_copy(text_proj, proj, local_sem.at[1]).start()

    barrier = pltpu.get_barrier_semaphore()
    known = {(axis, step, flip): along(axis, step, flip) for axis in range(3) for step in (1, 2, 3) for flip in (False, True)}
    partners = list(known.values()) + [sibling]
    for partner in partners:
        pl.semaphore_signal(barrier, inc=1, device_id=partner, device_id_type=MESH)
    pl.semaphore_wait(barrier, len(partners))

    def cross(src):
        return remote(src, feats.at[own], gather_send.at[14], gather_recv.at[1], sibling)

    @pl.when(is_image)
    def _():
        cross(text_feats).start()

    @pl.when(jnp.logical_not(is_image))
    def _():
        cross(image_feats).start()

    own_copy.wait()

    sends = {}
    for index, (path, to) in enumerate(((RING_UP, ring(1)), (RING_DOWN, ring(3)), (ACROSS, across))):
        for step, (source, target) in enumerate(path):
            sends[(index, step)] = remote(
                feats.at[slot(source)], feats.at[slot(target)], gather_send.at[index * 5 + step], arrival(target), to
            )

    def arrived(*key):
        remote(feats.at[slot(key)], feats.at[slot(key)], gather_send.at[0], arrival(key), sibling).wait_recv()

    sends[(0, 0)].start()
    sends[(1, 0)].start()
    arrived(0, 0, 1)
    sends[(2, 0)].start()
    sends[(0, 1)].start()
    sends[(1, 1)].start()
    sends[(2, 1)].start()
    proj_copy.wait()

    def unit_copy(index):
        rows = pl.ds(pl.multiple_of(index * UNIT, UNIT), UNIT)
        return remote(unit.at[rows], other.at[rows], unit_send.at[index], unit_recv.at[index], sibling)

    def project(index, buffer):
        rows = pl.ds(pl.multiple_of(index * UNIT, UNIT), UNIT)
        buffer[pl.ds(0, UNIT), :] = jnp.dot(feats[rows, :], proj[...], preferred_element_type=F32)
        feats_t[:, rows] = feats[rows, :].T

    def normalize(index, buffer):
        for i in range(UNIT // STEP):
            there = pl.ds(pl.multiple_of(index * UNIT + i * STEP, STEP), STEP)
            raw = buffer[pl.ds(i * STEP, STEP), :]
            inv = 1.0 / jnp.sqrt(jnp.sum(raw * raw, axis=1, keepdims=True) + 1e-06)
            value = raw * inv
            half = value.astype(BF16)
            unit[there, :] = half
            unit_low[there, :] = (value - half.astype(F32)).astype(BF16)
            inv_norm[there, :] = inv

    def three_units(units, ready):
        project(units[0], wide)
        project(units[1], perm)
        normalize(units[0], wide)
        unit_copy(units[0]).start()
        normalize(units[1], perm)
        unit_copy(units[1]).start()
        for key in ready:
            arrived(*key)
        project(units[2], wide)
        normalize(units[2], wide)
        unit_copy(units[2]).start()

    scale = jnp.exp(jnp.full((1, TILE), log_scale[0], F32))
    slope = scale * LOG2E
    offset = jnp.full((1, TILE), logit_bias[0], F32) * LOG2E

    def tile_copy(t, a, b):
        return remote(
            pairs_t.at[t],
            pairs.at[pl.ds(pl.multiple_of(b * TILE, TILE), TILE), pl.ds(pl.multiple_of(a * TILE, TILE), TILE)],
            tile_send.at[t], tile_recv.at[t], sibling,
        )

    def tile_place(t):
        place = []
        for k in range(2):
            found = [jnp.int32(TILES[c][7][k]) for c in range(2)]
            for i in range(7):
                found = [jnp.where(t == i, TILES[c][i][k], found[c]) for c in range(2)]
            place.append(jnp.where(is_image, found[0], found[1]))
        return place

    def cosines(t, buffer):
        a, b = tile_place(t)
        rows = pl.ds(pl.multiple_of(a * TILE, TILE), TILE)
        cols = pl.ds(pl.multiple_of(b * TILE, TILE), TILE)
        buffer[pl.ds(0, TILE), pl.ds(0, TILE)] = lax.dot_general(
            unit[rows, :], other[cols, :], (((1,), (1,)), ((), ())), preferred_element_type=F32
        )

    def pair_terms(t, buffer, diagonal):
        a, b = tile_place(t)
        cols = pl.ds(pl.multiple_of(b * TILE, TILE), TILE)
        acc = [jnp.zeros((8, TILE), F32) for _ in range(3)]
        for i in range(TILE // STEP):
            cosine = buffer[pl.ds(i * STEP, STEP), pl.ds(0, TILE)]
            arg = cosine * slope + offset
            masked = diagonal and i < UNIT // STEP
            if masked:
                row = i * STEP + lax.broadcasted_iota(jnp.int32, (STEP, TILE), 0)
                col = lax.broadcasted_iota(jnp.int32, (STEP, TILE), 1) + core * ROWS
                sign = jnp.where(row == col, -1.0, 1.0).astype(F32)
                arg = arg * sign
            up = jnp.exp2(arg)
            whole = 1.0 + up
            inv = pl.reciprocal(whole, approx=True)
            inv = inv * (2.0 - whole * inv)
            grad = up * inv
            loss = jnp.log(whole) + (up - (whole - 1.0)) * inv
            if masked:
                grad = grad * sign
            pairs[pl.ds(pl.multiple_of(a * TILE + i * STEP, STEP), STEP), cols] = grad.astype(BF16)
            acc = [acc[0] + fold(loss), acc[1] + fold(grad * cosine), acc[2] + fold(grad)]
        for k in range(3):
            sums[k] += acc[k]

    def hand_over(t):
        a, b = tile_place(t)
        rows = pl.ds(pl.multiple_of(a * TILE, TILE), TILE)
        cols = pl.ds(pl.multiple_of(b * TILE, TILE), TILE)
        pairs_t[t] = pairs[rows, cols].T
        tile_copy(t, a, b).start()

    def two_tiles(i, carry):
        t = 2 * i
        cosines(t + 1, perm)
        pair_terms(t, wide, False)
        hand_over(t)

        @pl.when(i == 1)
        def _():
            for index in range(6, 8):
                unit_copy(index).wait_recv()

        cosines(t + 2, wide)
        pair_terms(t + 1, perm, False)
        hand_over(t + 1)
        return carry

    sums[...] = jnp.zeros_like(sums)
    project(0, wide)
    normalize(0, wide)
    unit_copy(0).start()
    arrived(0, 3, 0)
    sends[(0, 2)].start()
    sends[(2, 2)].start()
    arrived(0, 1, 0)
    sends[(2, 3)].start()
    arrived(1, 0, 1)
    sends[(1, 2)].start()
    sends[(0, 3)].start()
    arrived(0, 1, 1)
    sends[(1, 3)].start()
    arrived(0, 3, 1)
    three_units((2, 3, 1), [(1, 0, 0)])
    arrived(1, 1, 1)
    sends[(1, 4)].start()
    arrived(1, 3, 0)
    sends[(0, 4)].start()
    for index in range(4):
        unit_copy(index).wait_recv()
    cosines(0, wide)
    cosines(1, perm)
    pair_terms(0, wide, True)
    hand_over(0)
    pair_terms(1, perm, False)
    hand_over(1)
    for key in ((1, 3, 1), (0, 2, 0), (0, 2, 1)):
        arrived(*key)
    three_units((4, 6, 5), [(1, 1, 0)])
    arrived(1, 2, 0)
    arrived(1, 2, 1)
    project(7, wide)
    normalize(7, wide)
    unit_copy(7).start()
    for index in range(4, 6):
        unit_copy(index).wait_recv()
    cosines(2, wide)
    lax.fori_loop(1, 3, two_tiles, 0)
    cosines(7, perm)
    pair_terms(6, wide, False)
    hand_over(6)
    pair_terms(7, perm, False)
    hand_over(7)

    def scalar_copies(stage):
        if stage == 3:
            return [remote(scalars.at[3, core], scalars.at[3, core], scalar_send.at[9], scalar_recv.at[9], sibling)]
        return [
            remote(
                scalars.at[stage, pos[stage]], scalars.at[stage, pos[stage]],
                scalar_send.at[stage * 3 + step - 1], scalar_recv.at[stage * 3 + step - 1], along(stage, step),
            )
            for step in (1, 2, 3)
        ]

    def scalar_start(stage, value):
        scalars[stage, pos[stage] if stage < 3 else core] = value
        for copy in scalar_copies(stage):
            copy.start()

    def scalar_finish(stage):
        for copy in scalar_copies(stage):
            copy.wait()
        if stage == 3:
            return scalars[3, 0] + scalars[3, 1]
        return (scalars[stage, 0] + scalars[stage, 1]) + (scalars[stage, 2] + scalars[stage, 3])

    lanes = [sums[k][:, 0:128] + sums[k][:, 128:256] + (sums[k][:, 256:384] + sums[k][:, 384:512]) for k in range(3)]
    scalar_start(0, jnp.concatenate(lanes, axis=0))

    for copy in sends.values():
        copy.wait_send()
    cross(text_feats).wait_send()
    for t in range(6):
        tile_copy(t, 0, 0).wait_recv()

    scale_row = jnp.exp(jnp.full((1, 1), log_scale[0], F32))

    def gradients(a, buffer):
        rows = pl.ds(pl.multiple_of(a * TILE, TILE), TILE)
        buffer[pl.ds(0, TILE), :] = jnp.dot(pairs[rows, :], other[...], preferred_element_type=F32)

    def tangents(a, buffer):
        for i in range(TILE // STEP):
            there = pl.ds(pl.multiple_of(a * TILE + i * STEP, STEP), STEP)
            grad = buffer[pl.ds(i * STEP, STEP), :]
            value = unit[there, :].astype(F32) + unit_low[there, :].astype(F32)
            inner = jnp.sum(value * grad, axis=1, keepdims=True)
            feats[there, :] = ((grad - value * inner) * (inv_norm[there, :] * scale_row)).astype(BF16)

    order = (1 - core, 3 - core, core, 2 + core)
    gradients(order[0], wide)
    gradients(order[1], perm)
    tangents(order[0], wide)
    for t in range(6, 8):
        tile_copy(t, 0, 0).wait_recv()
    gradients(order[2], wide)
    tangents(order[1], perm)
    gradients(order[3], perm)
    tangents(order[2], wide)
    tangents(order[3], perm)
    scalar_start(1, scalar_finish(0))

    def weights(parts):
        cols = pl.ds(parts[0] * PART, len(parts) * PART)
        wide[:, cols] = jnp.dot(feats_t[...], feats[:, cols], preferred_element_type=F32)

    up = 1 - 2 * core

    def columns(q):
        return pl.ds(q * PART, PART)

    def first_copies(q):
        axis = ORDERS[q % 3][0]
        ahead, behind = along(axis, lax.rem(4 + up, 4)), along(axis, lax.rem(4 - up, 4))
        return (
            remote(first_a.at[q], into_a.at[q], first_send.at[q, 0], first_recv.at[q, 0], ahead),
            remote(first_b.at[q], into_b.at[q], first_send.at[q, 1], first_recv.at[q, 1], behind),
            remote(into_a.at[q], into_c.at[q], first_send.at[q, 2], first_recv.at[q, 2], ahead),
        )

    def block(q, step):
        k = lax.rem(pos[ORDERS[q % 3][0]] + 4 + step, 4)
        return pl.ds(pl.multiple_of(k * 288, 288), 288), columns(q)

    def first_start(q):
        for k1 in range(4):
            for k2 in range(4):
                for k3 in range(4):
                    place = [0, 0, 0]
                    for axis, k in zip(ORDERS[q % 3], (k1, k2, k3)):
                        place[axis] = k
                    perm[pl.ds(k1 * 288 + k2 * 72 + k3 * 18, 18), columns(q)] = (
                        wide[pl.ds(natural_row(*place), 18), columns(q)])
        first_a[q] = perm[block(q, 2)].astype(BF16)
        first_b[q] = perm[block(q, -up)].astype(BF16)
        copies = first_copies(q)
        copies[0].start()
        copies[1].start()

    def first_forward(q):
        copies = first_copies(q)
        copies[0].wait_recv()
        into_a[q] = (perm[block(q, up)] + into_a[q].astype(F32)).astype(BF16)
        copies[2].start()

    def second_copies(b):
        start, size = SECOND[b]
        return [
            remote(second_out.at[step - 1, pl.ds(start, size)], second_in.at[step - 1, pl.ds(start, size)],
                   second_send.at[b, step - 1], second_recv.at[b, step - 1], known[ORDERS[BATCHES[b][0] % 3][1], step, False])
            for step in (1, 2, 3)
        ]

    def second_rows(q, step):
        return pl.ds(pl.multiple_of(lax.rem(pos[ORDERS[q % 3][1]] + step, 4) * 72, 8), 72)

    def second_start(b):
        for i, q in enumerate(BATCHES[b]):
            copies = first_copies(q)
            copies[1].wait_recv()
            copies[2].wait_recv()
            part_sum[q] = perm[block(q, 0)] + into_b[q].astype(F32) + into_c[q].astype(F32)
            for step in (1, 2, 3):
                second_out[step - 1, pl.ds(SECOND[b][0] + 80 * i, 72), :] = part_sum[q, second_rows(q, step), :].astype(BF16)
        for copy in second_copies(b):
            copy.start()

    def third_copies(b):
        axis = ORDERS[BATCHES[b][0] % 3][2]
        rows = pl.ds(*THIRD[b])
        copies = []
        for flip in (False, True):
            half = 1 - core if flip else core
            for step in range(4):
                if step or flip:
                    sem = 3 + step if flip else step - 1
                    copies.append(remote(
                        third_own.at[lax.rem(pos[axis] + step, 4), half, rows], third_in.at[core, step, rows],
                        third_send.at[b, sem], third_recv.at[b, sem], known[axis, step, flip] if step else sibling))
        return copies

    def third_start(b):
        for copy in second_copies(b):
            copy.wait_recv()
        for i, q in enumerate(BATCHES[b]):
            total = part_sum[q, second_rows(q, 0), :]
            for step in (1, 2, 3):
                total += second_in[step - 1, pl.ds(SECOND[b][0] + 80 * i, 72), :].astype(F32)
            part_sum[q, pl.ds(0, 72), :] = total
            for k in range(4):
                for h in range(2):
                    third_own[k, h, pl.ds(THIRD[b][0] + 9 * i, 9), :] = part_sum[q, pl.ds(18 * k + 9 * h, 9), :]
        for copy in third_copies(b):
            copy.start()
        rows = pl.ds(*THIRD[b])
        third_in[core, 0, rows] = third_own[pos[ORDERS[BATCHES[b][0] % 3][2]], core, rows]

    def third_finish(b):
        for copy in third_copies(b):
            copy.wait_recv()
        for i, q in enumerate(BATCHES[b]):
            for side in range(2):
                got = [third_in[side, step, pl.ds(THIRD[b][0] + 9 * i, 9), :] for step in range(4)]
                out[pl.ds(16 * side, 9), columns(q)] = (got[0] + got[1]) + (got[2] + got[3])

    def each(step, parts):
        for q in parts:
            step(q)

    early, middle, late = range(0, 4), range(4, 8), range(8, 9)
    weights(early)
    each(first_start, early)
    weights(middle)
    each(first_start, middle)
    each(first_forward, early)
    weights(late)
    each(first_start, late)
    each(first_forward, middle)
    scalar_start(2, scalar_finish(1))
    each(first_forward, late)
    each(second_start, range(0, 3))
    each(second_start, range(3, 4))
    scalar_start(3, scalar_finish(2))
    each(third_start, range(0, 3))
    each(third_start, range(3, 4))
    totals = scalar_finish(3)
    batch = 1.0 / 16384.0
    row_scale = jnp.exp(jnp.full((8, 128), log_scale[0], F32))
    for k, value in enumerate((totals[0:8], totals[8:16] * row_scale, totals[16:24])):
        out[pl.ds(9 + k, 1), pl.ds(0, 128)] = jnp.full((1, 128), jnp.sum(value) * batch, F32)
    each(third_finish, range(4))

    for q in range(9):
        for copy in first_copies(q):
            copy.wait_send()
    for b in range(4):
        for copy in second_copies(b) + third_copies(b):
            copy.wait_send()
    for index in range(8):
        unit_copy(index).wait_send()
        tile_copy(index, 0, 0).wait_send()

def split(packed, loss_out, image_out, text_out, scale_out, bias_out):
    image_out[...] = packed[pl.ds(0, 9), :]
    text_out[...] = packed[pl.ds(16, 9), :]
    loss_out[0] = packed[9, 0]
    scale_out[0] = packed[10, 0]
    bias_out[0] = packed[11, 0]


def per_device(image_feats, text_feats, image_proj, text_proj, log_scale, logit_bias):
    smem = pl.BlockSpec(memory_space=pltpu.SMEM)
    vmem = pl.BlockSpec(memory_space=pltpu.VMEM)
    hbm = pl.BlockSpec(memory_space=pl.ANY)
    dma, buffer = pltpu.SemaphoreType.DMA, pltpu.VMEM
    one = jax.ShapeDtypeStruct((1,), F32)
    rows = jax.ShapeDtypeStruct((9, WIDTH), F32)
    packed = pl.pallas_call(
        kernel,
        out_shape=jax.ShapeDtypeStruct((32, WIDTH), F32),
        in_specs=[smem, smem, hbm, hbm, hbm, hbm],
        out_specs=vmem,
        scratch_shapes=[
            buffer((ROWS, WIDTH), BF16),
            buffer((WIDTH, ROWS), BF16),
            buffer((ROWS, WIDTH), BF16),
            buffer((ROWS, WIDTH), BF16),
            buffer((ROWS, WIDTH), BF16),
            buffer((ROWS, ROWS), BF16),
            buffer((8, TILE, TILE), BF16),
            buffer((WIDTH, WIDTH), BF16),
            buffer((ROWS, 1), F32),
            buffer((WIDTH, WIDTH), F32),
            buffer((WIDTH, WIDTH), F32),
            buffer((3, 8, TILE), F32),
            *[buffer((9, 288, PART), BF16) for _ in range(5)],
            buffer((9, 288, PART), F32),
            buffer((3, 720, PART), BF16),
            buffer((3, 720, PART), BF16),
            buffer((4, 2, 104, PART), F32),
            buffer((2, 4, 104, PART), F32),
            buffer((4, 4, 24, 128), F32),
            dma((2,)),
            dma((15,)), dma((16,)),
            dma((8,)), dma((8,)),
            dma((8,)), dma((8,)),
            dma((9, 3)), dma((9, 3)), dma((4, 3)), dma((4, 3)), dma((4, 7)), dma((4, 7)),
            dma((10,)), dma((10,)),
        ],
        compiler_params=pltpu.CompilerParams(collective_id=0, has_side_effects=True, vmem_limit_bytes=63 * 2**20),
        name="sigmoid_loss",
    )(log_scale, logit_bias, image_feats, text_feats, image_proj, text_proj)
    return pl.pallas_call(
        split,
        out_shape=(one, rows, rows, one, one),
        in_specs=[vmem],
        out_specs=(smem, vmem, vmem, smem, smem),
        name="split_outputs",
    )(packed)


def solution(mesh):
    return jax.shard_map(
        per_device,
        mesh=mesh,
        in_specs=(P(("dp", "mp"), None), P(("dp", "mp"), None), P(), P(), P(), P()),
        out_specs=(P(), P(("dp", "mp"), None), P(("dp", "mp"), None), P(), P()),
        check_vma=False,
    )
```
